256 devices in a mesh: chol: 16 (over x_lo, y, core), walk: 16 (over x_hi, z).
Axes of the slice: x: 4 (x_hi: 2, x_lo: 2; x = x_hi * 2 + x_lo), y: 4, z: 8, core: 2. Of those that a mesh axis runs over, the one named last changes fastest.
Arguments:
- trial: float32 [80, 400], replicated, as said below
- walkers: float32 [512, 80, 400], P(('chol', 'walk')), as said below
- aux_field: float32 [512, 2400], P(None, 'chol'), may hold values from -6 to 6
- half_rotated: bfloat16 [2400, 32000], P('chol', 'walk'), may hold values from -0.625 to 0.625
- cholesky_vecs: bfloat16 [2400, 160000], P('chol', 'walk'), may hold values from -0.0078125 to 0.0078125
Outputs:
- next_walkers: float32 [512, 80, 400], P(('chol', 'walk'))
- force_bias: float32 [512, 2400], P(None, 'chol')
The draws below stay inside these ranges and needn't reach their ends.
Inputs may be any that keep to these rules, and one draw needn't show every extreme that they name: Row i of the trial orbitals is the i-th unit vector of length 400 plus a small dense perturbation. `walkers`: row i of each walker's orbitals is the i-th unit vector of length 400 plus a small dense perturbation.
All inputs are finite; a program needn't handle non-finite values.
Results may differ from the reference program's by a relative error of at most 0.0031.
Values may be sent and summed in bfloat16 or wider, within the bound.
A program may use at most 128 MiB of HBM per device.

```python
import jax
import jax.numpy as jnp
from jax import lax

M = 400
NE = 80
NCHOL = 2400
TAYLOR = 6
W = 512
N_CHOL = 16


def near_unit(key, leading, spread):
    noise = jnp.clip(jax.random.normal(key, leading + (NE, M), jnp.float32), -4.0, 4.0)
    rows = jnp.arange(NE)[:, None]
    cols = jnp.arange(M)[None, :]
    unit = (rows == cols).astype(jnp.float32)
    return unit + spread * noise / M ** 0.5


def draw_trial(key, part):
    key = jax.random.fold_in(key, 11)
    return near_unit(key, (), 0.6)


def draw_walkers(key, part):
    key = jax.random.fold_in(key, 23)
    return near_unit(key, (W,), 0.6)


def level_of(own_key, shape, cuts, smallest, high):
    loudness = 1.0
    for axis_at, shards_of in cuts:
        heights = jax.random.uniform(jax.random.fold_in(jax.random.fold_in(own_key, 6), axis_at), (shards_of,), jnp.float32, smallest / len(cuts), high / len(cuts))
        loudness = loudness * jnp.repeat(jnp.exp(heights), shape[axis_at] // shards_of).reshape((-1,) + (1,) * (len(shape) - 1 - axis_at))
    return loudness


def normal_values(own_key, extent, scale, limit, cuts=(), kind=jnp.bfloat16):
    result = scale * jax.random.normal(own_key, extent, jnp.float32)
    if cuts:
        result = result * level_of(own_key, extent, cuts, -0.22, 0.18)
    return jnp.clip(result, -limit, limit).astype(kind)


def setup_inputs(seed: int = 0) -> dict:
    key_list = jax.random.split(jax.random.key(seed), 6)
    trial = draw_trial(jax.random.fold_in(key_list[5], 71), 0)
    walkers = draw_walkers(jax.random.fold_in(key_list[5], 71), 0)
    aux_field = normal_values(key_list[2], (W, NCHOL), 1.0, 6.0, ((1, 16),), jnp.float32)
    half_rotated = normal_values(key_list[3], (NCHOL, NE * M), 100 ** -0.5, 0.625, ((0, 16), (1, 16)))
    cholesky_vecs = normal_values(key_list[4], (NCHOL, M * M), (0.5 / (M * NCHOL) ** 0.5), 0.0078125, ((0, 16), (1, 16)))
    return dict(trial=trial, walkers=walkers, aux_field=aux_field, half_rotated=half_rotated, cholesky_vecs=cholesky_vecs)


HIGH = lax.Precision.HIGHEST

def green_of(trial, walkers):
    correlation = jnp.einsum('ip,wjp->wij', trial, walkers, precision=HIGH)
    gram = jnp.einsum('wij,wkj->wik', correlation, correlation, precision=HIGH)
    rhs = jnp.einsum('wij,wjp->wip', correlation, walkers, precision=HIGH)
    factor = jnp.linalg.cholesky(gram)
    middle = lax.linalg.triangular_solve(factor, rhs, left_side=True, lower=True)
    return lax.linalg.triangular_solve(factor, middle, left_side=True, lower=True, transpose_a=True)

def taylor_step(walkers, onebody):
    term = walkers
    total = walkers
    for order in range(1, TAYLOR + 1):
        term = -jnp.einsum('wip,wqp->wiq', term, onebody, precision=HIGH) / order
        total = total + term
    return total

def reference(trial, walkers, aux_field, half_rotated, cholesky_vecs):
    count = walkers.shape[0]
    green = green_of(trial, walkers).reshape(count, NE * M).astype(jnp.bfloat16)
    force_bias = lax.dot_general(green.astype(jnp.float32), half_rotated.astype(jnp.float32), (((1,), (1,)), ((), ())), preferred_element_type=jnp.float32)
    field = (aux_field - force_bias).astype(jnp.bfloat16)
    field_blocks = field.reshape(N_CHOL, count // N_CHOL, NCHOL)
    walker_blocks = walkers.reshape(N_CHOL, count // N_CHOL, NE, M)

    def advance(pair):
        block_field, block_walkers = pair
        onebody = jnp.dot(block_field.astype(jnp.float32), cholesky_vecs.astype(jnp.float32), preferred_element_type=jnp.float32)
        onebody = onebody.reshape(block_field.shape[0], M, M)
        return taylor_step(block_walkers, onebody)
    next_walkers = lax.map(advance, (field_blocks, walker_blocks)).reshape(count, NE, M)
    return (next_walkers, force_bias)
```

```python
import functools

import jax
import jax.numpy as jnp
from jax import lax
from jax.experimental import pallas as pl
from jax.experimental.pallas import tpu as pltpu
from jax.sharding import PartitionSpec as P

TAYLOR = 6
HIGH = lax.Precision.HIGHEST
MESH = pl.DeviceIdType.MESH
F32 = jnp.float32
BF16 = jnp.bfloat16
SLOT = 16


def up(value, multiple):
    return -(-value // multiple) * multiple


def iota(shape, dim):
    return lax.broadcasted_iota(jnp.int32, shape, dim)


def permutation(rows, cols, source):
    return jnp.where(iota((rows, cols), 1) == source(iota((rows, cols), 0)), 1.0, 0.0).astype(BF16)


def dot(a, b, contract=((1,), (0,)), precision=None):
    return lax.dot_general(a, b, (contract, ((), ())), preferred_element_type=F32, precision=precision)


def invert(grams):
    size = grams[0].shape[0]
    rows = iota((size, 1), 0)
    lanes = iota((1, size), 1)
    mats = list(grams)
    for k in range(size):
        for n, a in enumerate(mats):
            col = a[:, k : k + 1]
            row = a[k : k + 1, :]
            inv = 1.0 / a[k : k + 1, k : k + 1]
            row = jnp.where(lanes == k, inv, row * inv)
            col = jnp.where(rows == k, -1.0, col)
            kept = jnp.where((lanes == k) | (rows == k), 0.0, a)
            mats[n] = kept - col * row
    return mats


def green_kernel(parts, trial_ref, walkers_ref, out_ref):
    count, electrons, _ = walkers_ref.shape
    each = electrons // parts
    trial = trial_ref[...]
    walkers = [walkers_ref[j] for j in range(count)]
    corr = [dot(trial, w, ((1,), (1,)), HIGH) for w in walkers]
    grams = [dot(c, c, ((1,), (1,)), HIGH) for c in corr]
    inverse = invert(grams)
    green = [dot(g, dot(c, w, precision=HIGH), precision=HIGH).astype(BF16) for g, c, w in zip(inverse, corr, walkers)]
    total = None
    for j in range(count):

        def source(r):
            inside = r % SLOT - each * j
            return jnp.where((inside >= 0) & (inside < each), (r // SLOT) * each + inside, -1)

        part = dot(permutation(parts * SLOT, electrons, source), green[j])
        total = part if total is None else total + part
    out_ref[...] = total.astype(BF16)


def exchange_kernel(
    dims,
    green_ref,
    hr_ref,
    aux_ref,
    vecs_ref,
    result_ref,
    bias_ref,
    hr_buf,
    aux_buf,
    vecs_buf,
    first_buf,
    wide_f32,
    entries,
    partial,
    partial_in,
    piece_f,
    piece_b,
    fields,
    bias_in,
    bias_out,
    bias_sib,
    acc,
    out,
    one_in,
    two_out,
    one_sems,
    vec_sems,
    fwd_sems,
    first_sems,
    entry_sems,
    partial_sems,
    field_w_sems,
    field_c_sems,
    bias_sems,
    hop1_sems,
    hop2_sems,
):
    k_count, w_count, owned, each, orbitals, vec_count = dims
    c = lax.axis_index("chol")
    w = lax.axis_index("walk")
    core = lax.rem(c, 2)
    k = lax.div(c, 2)
    other = 1 - core
    sibling = (2 * k + other, w)
    gp = hr_ref.shape[0]
    width = vecs_buf.shape[-1]
    rows = k_count * w_count * owned
    per_k = w_count * owned
    per_w = k_count * owned

    def at_k(kk):
        return (2 * kk + core, w)

    def at_w(ww):
        return (c, ww)

    def remote(src, dst, sems, slot, device):
        return pltpu.make_async_remote_copy(
            src_ref=src, dst_ref=dst, send_sem=sems.at[0, slot], recv_sem=sems.at[1, slot], device_id=device, device_id_type=MESH
        )

    def each_of(count, body):
        def step(d, carry):
            body(d)
            return carry

        lax.fori_loop(1, count, step, 0)

    def to_k(d):
        return lax.rem(k + d, k_count)

    def from_k(d):
        return lax.rem(k - d + k_count, k_count)

    def to_w(d):
        return lax.rem(w + d, w_count)

    def from_w(d):
        return lax.rem(w - d + w_count, w_count)

    def piece_start(which):
        first = per_w * w
        return per_k * (2 * lax.div(first, per_k) + which) + lax.rem(first, per_k)

    barrier = pltpu.get_barrier_semaphore()
    each_of(k_count, lambda d: pl.semaphore_signal(barrier, inc=1, device_id=at_k(to_k(d)), device_id_type=MESH))
    each_of(w_count, lambda d: pl.semaphore_signal(barrier, inc=1, device_id=at_w(to_w(d)), device_id_type=MESH))
    pl.semaphore_signal(barrier, inc=1, device_id=sibling, device_id_type=MESH)
    pl.semaphore_wait(barrier, k_count + w_count - 1)

    def first_copy(d):
        dst = to_w(d)
        return remote(green_ref.at[pl.ds(pl.multiple_of(dst * SLOT, SLOT), SLOT)], first_buf.at[w], first_sems, d, at_w(dst))

    each_of(w_count, lambda d: first_copy(d).start())
    first_buf[w] = green_ref[pl.ds(pl.multiple_of(w * SLOT, SLOT), SLOT), :]

    hr_copy = remote(hr_ref, hr_buf.at[core], one_sems, 0, sibling)
    hr_own = pltpu.make_async_copy(hr_ref, hr_buf.at[core], one_sems.at[2, 0])
    hr_copy.start()
    hr_own.start()
    aux_copy = remote(aux_ref.at[pl.ds(pl.multiple_of(piece_start(other), per_w), per_w)], aux_buf.at[core], one_sems, 1, sibling)
    aux_copy.start()
    aux_buf[core] = aux_ref[pl.ds(pl.multiple_of(piece_start(core), per_w), per_w), :]

    def vec_copy(d):
        dst = to_k(d)
        return remote(vecs_ref.at[:, pl.ds(pl.multiple_of(dst * width, 128), width)], vecs_buf.at[k, core], vec_sems, d, at_k(dst))

    vec_own = pltpu.make_async_copy(vecs_ref.at[:, pl.ds(pl.multiple_of(k * width, 128), width)], vecs_buf.at[k, core], one_sems.at[2, 1])
    vec_own.start()
    each_of(k_count, lambda d: vec_copy(d).start())

    each_of(w_count, lambda d: first_copy(d).wait_recv())
    slots = first_buf[...].reshape(w_count * SLOT, orbitals)
    pick = permutation(
        each * per_k,
        w_count * SLOT,
        lambda r: lax.rem(r, per_k) // owned * SLOT + lax.rem(r, owned) * each + lax.div(r, per_k),
    )
    picked = dot(pick, slots)
    wide_f32[...] = jnp.zeros_like(wide_f32)
    for i in range(each):
        wide_f32[:, i * orbitals : (i + 1) * orbitals] = picked[i * per_k : (i + 1) * per_k, :]
    entries[k] = wide_f32[...].astype(BF16)

    def entry_copy(d):
        return remote(entries.at[k], entries.at[k], entry_sems, d, at_k(to_k(d)))

    each_of(k_count, lambda d: entry_copy(d).start())
    hr_own.wait()
    hr_copy.wait_recv()
    each_of(k_count, lambda d: remote(entries.at[from_k(d)], entries.at[from_k(d)], entry_sems, d, at_k(to_k(d))).wait_recv())
    partial[...] = dot(
        entries[...].reshape(rows, entries.shape[-1]), hr_buf[...].reshape(2 * gp, entries.shape[-1]), ((1,), (1,))
    )

    def partial_copy(d):
        dst = to_w(d)
        return remote(partial.at[pl.ds(pl.multiple_of(dst * per_w, per_w), per_w)], partial_in.at[w], partial_sems, d, at_w(dst))

    each_of(w_count, lambda d: partial_copy(d).start())
    partial_in[w] = partial[pl.ds(pl.multiple_of(w * per_w, per_w), per_w), :]
    aux_copy.wait_recv()
    aux = jnp.concatenate([aux_buf[0], aux_buf[1]], axis=1)
    each_of(w_count, lambda d: partial_copy(d).wait_recv())
    bias = jnp.sum(partial_in[...], axis=0)
    piece_b[...] = bias
    piece_f[...] = (aux - bias).astype(BF16)

    my_rows = pl.ds(pl.multiple_of(w * per_w, per_w), per_w)

    def field_copy(d):
        return remote(piece_f, fields.at[k, my_rows], field_w_sems, d, at_w(to_w(d)))

    each_of(w_count, lambda d: field_copy(d).start())
    fields[k, my_rows, :] = piece_f[...]

    def bias_copy(d):
        return remote(piece_b, bias_in.at[my_rows], bias_sems, d, at_w(to_w(d)))

    each_of(w_count, lambda d: field_copy(d).wait_recv())

    def fields_copy(d):
        return remote(fields.at[k], fields.at[k], field_c_sems, d, at_k(to_k(d)))

    each_of(k_count, lambda d: fields_copy(d).start())
    each_of(w_count, lambda d: bias_copy(d).start())
    bias_in[my_rows, :] = piece_b[...]

    def forward_copy(kk):
        return remote(vecs_buf.at[kk, core], vecs_buf.at[kk, core], fwd_sems, kk, sibling)

    vec_own.wait()
    forward_copy(k).start()

    def forward(d):
        vec_copy(d).wait_recv()
        forward_copy(from_k(d)).start()

    each_of(k_count, forward)

    def forward_in(kk):
        return remote(vecs_buf.at[kk, other], vecs_buf.at[kk, other], fwd_sems, kk, sibling)

    forward_in(k).wait_recv()
    acc[...] = dot(fields[k], vecs_buf[k].reshape(2 * gp, width))

    def add(d):
        kk = from_k(d)
        remote(fields.at[kk], fields.at[kk], field_c_sems, d, at_k(to_k(d))).wait_recv()
        forward_in(kk).wait_recv()
        acc[...] += dot(fields[kk], vecs_buf[kk].reshape(2 * gp, width))

    each_of(k_count, add)
    out[...] = acc[...].astype(BF16)

    def hop1(d):
        dst = to_k(d)
        return remote(out.at[pl.ds(pl.multiple_of(dst * per_k, per_k), per_k)], one_in.at[k], hop1_sems, d, at_k(dst))

    each_of(k_count, lambda d: hop1(d).start())
    one_in[k] = out[pl.ds(pl.multiple_of(k * per_k, per_k), per_k), :]

    each_of(w_count, lambda d: bias_copy(d).wait_recv())
    low, high = bias_in[:, :gp], bias_in[:, gp:]
    bias_out[...] = jnp.where(core == 0, high, low)
    sib_copy = remote(bias_out, bias_sib, one_sems, 2, sibling)
    sib_copy.start()
    mine = jnp.where(core == 0, low, high)[:, :vec_count]
    for kk in range(k_count):
        start = pl.multiple_of((2 * kk + core) * per_k, per_k)
        bias_ref[pl.ds(start, per_k), :] = mine[kk * per_k : (kk + 1) * per_k]

    each_of(k_count, lambda d: hop1(d).wait_recv())
    regroup = permutation(rows, rows, lambda r: lax.rem(lax.div(r, owned), k_count) * per_k + lax.div(r, per_w) * owned + lax.rem(r, owned))
    two_out[...] = dot(regroup, one_in[...].reshape(rows, width)).astype(BF16)

    def hop2(d):
        dst = to_w(d)
        return remote(two_out.at[pl.ds(pl.multiple_of(dst * per_w, per_w), per_w)], result_ref.at[w], hop2_sems, d, at_w(dst))

    each_of(w_count, lambda d: hop2(d).start())
    result_ref[w] = two_out[pl.ds(pl.multiple_of(w * per_w, per_w), per_w), :]
    sib_copy.wait_recv()
    theirs = bias_sib[:, :vec_count]
    for kk in range(k_count):
        start = pl.multiple_of((2 * kk + other) * per_k, per_k)
        bias_ref[pl.ds(start, per_k), :] = theirs[kk * per_k : (kk + 1) * per_k]

    each_of(w_count, lambda d: hop2(d).wait_recv())

    hr_copy.wait_send()
    aux_copy.wait_send()
    sib_copy.wait_send()
    forward_copy(k).wait_send()

    def drain_k(d):
        vec_copy(d).wait_send()
        forward_copy(from_k(d)).wait_send()
        entry_copy(d).wait_send()
        fields_copy(d).wait_send()
        hop1(d).wait_send()

    def drain_w(d):
        first_copy(d).wait_send()
        partial_copy(d).wait_send()
        field_copy(d).wait_send()
        bias_copy(d).wait_send()
        hop2(d).wait_send()

    each_of(k_count, drain_k)
    each_of(w_count, drain_w)


def taylor_kernel(k_count, walkers_ref, pieces_ref, out_ref, flat, stacked):
    owned, _, orbitals = walkers_ref.shape
    w_count, per_w, width = pieces_ref.shape
    each = orbitals // w_count
    rows = w_count * per_w
    order = permutation(
        rows, rows, lambda r: lax.rem(r, w_count) * per_w + lax.rem(lax.div(r, w_count), k_count) * owned + lax.div(r, w_count * k_count)
    )
    sorted_ = dot(order, pieces_ref[...].reshape(rows, width))
    place = permutation(orbitals, orbitals, lambda r: lax.rem(r, each) * w_count + lax.div(r, each))
    terms, totals, onebody = [], [], []
    for j in range(owned):
        for kk in range(k_count):
            at = (j * k_count + kk) * w_count
            flat[j, :, kk * width : (kk + 1) * width] = sorted_[at : at + w_count, :]
        for q in range(each):
            stacked[j, q * w_count : (q + 1) * w_count, :] = flat[j, :, q * orbitals : (q + 1) * orbitals].astype(BF16)
        onebody.append(dot(stacked[j], place, ((0,), (1,))).astype(BF16))
        terms.append(walkers_ref[j])
        totals.append(walkers_ref[j])
    for step in range(1, TAYLOR + 1):
        for j in range(owned):
            head = terms[j].astype(BF16)
            rest = (terms[j] - head.astype(F32)).astype(BF16)
            terms[j] = (dot(head, onebody[j]) + dot(rest, onebody[j])) * (-1.0 / step)
            totals[j] = totals[j] + terms[j]
    for j in range(owned):
        out_ref[j] = totals[j]


def body(trial, walkers, aux_field, half_rotated, cholesky_vecs):
    k_count = lax.axis_size("chol") // 2
    w_count = lax.axis_size("walk")
    owned, electrons, orbitals = walkers.shape
    vec_count, local_entries = half_rotated.shape
    walker_count = aux_field.shape[0]
    local_pairs = cholesky_vecs.shape[1]
    each = electrons // w_count
    gp = up(vec_count, 16)
    lanes = up(local_entries, 128)
    width = up(-(-local_pairs // k_count), 128)
    rows = k_count * w_count * owned
    per_k, per_w = w_count * owned, k_count * owned
    vmem = pl.BlockSpec(memory_space=pltpu.VMEM)
    anywhere = pl.BlockSpec(memory_space=pl.ANY)

    green = pl.pallas_call(
        functools.partial(green_kernel, w_count),
        out_shape=jax.ShapeDtypeStruct((w_count * SLOT, orbitals), BF16),
        in_specs=[vmem, vmem],
        out_specs=vmem,
    )(trial, walkers)

    hr = jnp.pad(half_rotated, ((0, gp - vec_count), (0, lanes - local_entries)))
    vecs = jnp.pad(cholesky_vecs, ((0, gp - vec_count), (0, k_count * width - local_pairs)))
    aux = jnp.pad(aux_field, ((0, 0), (0, gp - vec_count)))
    dma = pltpu.SemaphoreType.DMA
    pieces, force_bias = pl.pallas_call(
        functools.partial(exchange_kernel, (k_count, w_count, owned, each, orbitals, vec_count)),
        out_shape=(
            jax.ShapeDtypeStruct((w_count, per_w, width), BF16),
            jax.ShapeDtypeStruct((walker_count, vec_count), F32),
        ),
        in_specs=[vmem, anywhere, vmem, anywhere],
        out_specs=(vmem, vmem),
        scratch_shapes=[
            pltpu.VMEM((2, gp, lanes), BF16),
            pltpu.VMEM((2, per_w, gp), F32),
            pltpu.VMEM((k_count, 2, gp, width), BF16),
            pltpu.VMEM((w_count, SLOT, orbitals), BF16),
            pltpu.VMEM((per_k, lanes), F32),
            pltpu.VMEM((k_count, per_k, lanes), BF16),
            pltpu.VMEM((rows, 2 * gp), F32),
            pltpu.VMEM((w_count, per_w, 2 * gp), F32),
            pltpu.VMEM((per_w, 2 * gp), BF16),
            pltpu.VMEM((per_w, 2 * gp), F32),
            pltpu.VMEM((k_count, rows, 2 * gp), BF16),
            pltpu.VMEM((rows, 2 * gp), F32),
            pltpu.VMEM((rows, gp), F32),
            pltpu.VMEM((rows, gp), F32),
            pltpu.VMEM((rows, width), F32),
            pltpu.VMEM((rows, width), BF16),
            pltpu.VMEM((k_count, per_k, width), BF16),
            pltpu.VMEM((rows, width), BF16),
            dma((3, 3)),
            dma((2, k_count)),
            dma((2, k_count)),
            dma((2, w_count)),
            dma((2, k_count)),
            dma((2, w_count)),
            dma((2, w_count)),
            dma((2, k_count)),
            dma((2, w_count)),
            dma((2, k_count)),
            dma((2, w_count)),
        ],
        compiler_params=pltpu.CompilerParams(collective_id=0, has_side_effects=True, vmem_limit_bytes=48 * 1024 * 1024),
    )(green, hr, aux, vecs)

    next_walkers = pl.pallas_call(
        functools.partial(taylor_kernel, k_count),
        out_shape=jax.ShapeDtypeStruct(walkers.shape, F32),
        in_specs=[vmem, vmem],
        out_specs=vmem,
        scratch_shapes=[
            pltpu.VMEM((owned, w_count, k_count * width), F32),
            pltpu.VMEM((owned, orbitals, orbitals), BF16),
        ],
        compiler_params=pltpu.CompilerParams(vmem_limit_bytes=32 * 1024 * 1024),
    )(walkers, pieces)
    return (next_walkers, force_bias)


def solution(mesh):
    in_specs = (
        P(),
        P(("chol", "walk"), None, None),
        P(None, "chol"),
        P("chol", "walk"),
        P("chol", "walk"),
    )
    out_specs = (P(("chol", "walk"), None, None), P(None, "chol"))
    return jax.shard_map(body, mesh=mesh, in_specs=in_specs, out_specs=out_specs, check_vma=False)
```

```python
import functools

import jax
import jax.numpy as jnp
from jax import lax
from jax.experimental import pallas as pl
from jax.experimental.pallas import tpu as pltpu
from jax.sharding import PartitionSpec as P

TAYLOR = 6
SIDE, LINE = 2, 4
CHUNKS = 2
HIGH = lax.Precision.HIGHEST
MESH = pl.DeviceIdType.MESH
F32 = jnp.float32
BF16 = jnp.bfloat16
SLOT = 16


def up(value, multiple):
    return -(-value // multiple) * multiple


def iota(shape, dim):
    return lax.broadcasted_iota(jnp.int32, shape, dim)


def permutation(rows, cols, source):
    return jnp.where(iota((rows, cols), 1) == source(iota((rows, cols), 0)), 1.0, 0.0).astype(BF16)


def dot(a, b, contract=((1,), (0,)), precision=None):
    return lax.dot_general(a, b, (contract, ((), ())), preferred_element_type=F32, precision=precision)


def invert(grams):
    size = grams[0].shape[0]
    rows = iota((size, 1), 0)
    lanes = iota((1, size), 1)

    def step(_, mats):
        mats = list(mats)
        for k in range(8):
            for n, a in enumerate(mats):
                col = a[:, k : k + 1]
                row = a[k : k + 1, :]
                inv = 1.0 / a[k : k + 1, k : k + 1]
                row = jnp.where(lanes == k, inv, row * inv)
                col = jnp.where(rows == k, -1.0, col)
                kept = jnp.where((lanes == k) | (rows == k), 0.0, a)
                mats[n] = kept - col * row
        mats = [jnp.concatenate([a[8:], a[:8]], axis=0) for a in mats]
        return tuple(jnp.concatenate([a[:, 8:], a[:, :8]], axis=1) for a in mats)

    return lax.fori_loop(0, size // 8, step, tuple(grams))


def blocks_of_green(parts, trial_ref, walkers_ref, before_inverse):
    count, electrons, _ = walkers_ref.shape
    each = electrons // parts
    trial = trial_ref[...]
    walkers = [walkers_ref[j] for j in range(count)]
    corr = [dot(trial, w, ((1,), (1,)), HIGH) for w in walkers]
    grams = [dot(c, c, ((1,), (1,)), HIGH) for c in corr]
    before_inverse()
    inverse = invert(grams)
    green = [dot(g, dot(c, w, precision=HIGH), precision=HIGH).astype(BF16) for g, c, w in zip(inverse, corr, walkers)]
    total = None
    for j in range(count):

        def source(r):
            inside = r % SLOT - each * j
            return jnp.where((inside >= 0) & (inside < each), (r // SLOT) * each + inside, -1)

        part = dot(permutation(parts * SLOT, electrons, source), green[j])
        total = part if total is None else total + part
    return total.astype(BF16)


def exchange_kernel(
    dims,
    trial_ref,
    walkers_ref,
    hr_ref,
    aux_ref,
    vecs_ref,
    result_ref,
    bias_ref,
    green,
    hr_buf,
    aux_out,
    aux_buf,
    vecs_out,
    vecs_buf,
    relay,
    first_buf,
    wide_f32,
    entries,
    partial,
    partial_in,
    piece_f,
    piece_b,
    fields,
    bias_in,
    bias_out,
    bias_sib,
    out,
    one_in,
    two_out,
    one_sems,
    vec_sems,
    fwd_sems,
    first_sems,
    entry_sems,
    partial_sems,
    field_w_sems,
    field_c_sems,
    bias_sems,
    hop1_sems,
    hop2_sems,
):
    k_count, w_count, owned, each, orbitals, vec_count = dims
    c = lax.axis_index("chol")
    w = lax.axis_index("walk")
    core = lax.rem(c, 2)
    k = lax.div(c, 2)
    other = 1 - core
    sibling = (2 * k + other, w)
    gp = hr_buf.shape[1]
    width = vecs_buf.shape[-1]
    part_width = width // CHUNKS
    rows = k_count * w_count * owned
    per_k = w_count * owned
    per_w = k_count * owned
    local_pairs = vecs_ref.shape[1]
    local_entries = hr_ref.shape[1]

    line = LINE * lax.div(k, LINE)
    across = lax.rem(k + LINE, k_count)
    line_across = lax.rem(line + LINE, k_count)

    def along(start, step):
        return start + lax.rem(k - line + step, LINE)

    fore, back, half = along(line, 1), along(line, LINE - 1), along(line, 2)
    fore_x, back_x, half_x = along(line_across, 1), along(line_across, LINE - 1), along(line_across, 2)

    def at_k(kk):
        return (2 * kk + core, w)

    def at_w(ww):
        return (c, ww)

    def remote(src, dst, sems, slot, device):
        return pltpu.make_async_remote_copy(
            src_ref=src, dst_ref=dst, send_sem=sems.at[0, slot], recv_sem=sems.at[1, slot], device_id=device, device_id_type=MESH
        )

    drains = []

    def start(copy):
        copy.start()
        drains.append(copy.wait_send)
        return copy

    def each_of(count, body):
        def step(d, carry):
            body(d)
            return carry

        lax.fori_loop(1, count, step, 0)

    def start_each(count, make):
        each_of(count, lambda d: make(d).start())
        drains.append(lambda: each_of(count, lambda d: make(d).wait_send()))

    def to_k(d):
        return lax.rem(k + d, k_count)

    def to_w(d):
        return lax.rem(w + d, w_count)

    def walker_of(row, which):
        return per_k * (2 * lax.div(row, per_k) + which) + lax.rem(row, per_k)

    def span(index, size):
        return pl.ds(pl.multiple_of(index * size, size), size)

    barrier = pltpu.get_barrier_semaphore()
    each_of(k_count, lambda d: pl.semaphore_signal(barrier, inc=1, device_id=at_k(to_k(d)), device_id_type=MESH))
    each_of(w_count, lambda d: pl.semaphore_signal(barrier, inc=1, device_id=at_w(to_w(d)), device_id_type=MESH))
    pl.semaphore_signal(barrier, inc=1, device_id=sibling, device_id_type=MESH)

    vecs_out[gp - 16 :, :] = jnp.zeros((16, vecs_out.shape[1]), BF16)
    edge = local_pairs // 128 * 128
    if edge < vecs_out.shape[1]:
        vecs_out[:, edge:] = jnp.zeros((gp, vecs_out.shape[1] - edge), BF16)
    vecs_out[:vec_count, :local_pairs] = vecs_ref[...]
    hr_buf[core] = jnp.zeros(hr_buf.shape[1:], BF16)
    hr_buf[core, :vec_count, :local_entries] = hr_ref[...]

    cut = gp // 2
    lower, upper = pl.ds(0, cut), pl.ds(cut, gp - cut)

    def vec_full(slot, dst, src):
        return remote(vecs_out.at[:, span(dst, width)], vecs_buf.at[src, core], vec_sems, slot, at_k(dst))

    def vec_lower(slot, dst, src):
        return remote(vecs_out.at[lower, span(dst, width)], vecs_buf.at[src, core, lower], vec_sems, slot, at_k(dst))

    def vec_relay(slot, dst, by):
        return remote(vecs_out.at[upper, span(dst, width)], relay.at[slot - 7], vec_sems, slot, at_k(by))

    def vec_upper(slot, dst, src):
        return remote(relay.at[slot - 9], vecs_buf.at[src, core, upper], vec_sems, slot, at_k(dst))

    def vec_forward(kk):
        return remote(vecs_buf.at[kk, core], vecs_buf.at[kk, core], fwd_sems, kk, sibling)

    def vec_from_sibling(kk):
        return remote(vecs_buf.at[kk, other], vecs_buf.at[kk, other], fwd_sems, kk, sibling)

    own_vecs = pltpu.make_async_copy(vecs_out.at[:, span(k, width)], vecs_buf.at[k, core], one_sems.at[2, 0])
    hr_copy = remote(hr_buf.at[core], hr_buf.at[core], one_sems, 0, sibling)
    aux_copy = remote(aux_out, aux_buf.at[core], one_sems, 1, sibling)

    def first_window():
        pl.semaphore_wait(barrier, k_count + w_count - 1)
        start(vec_relay(7, half, back))
        start(vec_relay(8, half_x, back))
        start(vec_full(2, across, k))
        start(vec_full(0, fore, k))
        start(vec_full(1, back, k))
        start(vec_full(3, fore_x, k))
        own_vecs.start()
        start(hr_copy)

    def second_window():
        vec_relay(7, half, back).wait_recv()
        start(vec_upper(9, back, fore))
        vec_relay(8, half_x, back).wait_recv()
        start(vec_upper(10, back_x, fore))
        start(vec_lower(5, half, k))
        start(vec_lower(6, half_x, k))
        start(vec_full(4, back_x, k))

    def finish_first_window():
        own_vecs.wait()
        start(vec_forward(k))
        for slot, src in ((2, across), (0, back), (1, fore), (3, back_x)):
            vec_full(slot, k, src).wait_recv()
            start(vec_forward(src))

    def finish_second_window():
        vec_full(4, k, fore_x).wait_recv()
        start(vec_forward(fore_x))
        for slots, src in (((5, 9), half), ((6, 10), half_x)):
            vec_lower(slots[0], k, src).wait_recv()
            vec_upper(slots[1], k, src).wait_recv()
            start(vec_forward(src))

    class Gather:
        def __init__(self, buf, sems, size):
            self.buf, self.sems = buf, sems
            self.halves = pl.ds(0, size // 2), pl.ds(size // 2, size - size // 2)

        def full(self, slot, src, dst):
            return remote(self.buf.at[src], self.buf.at[src], self.sems, slot, at_k(dst))

        def part(self, slot, src, dst):
            ref = self.buf.at[src, self.halves[slot % 2]]
            return remote(ref, ref, self.sems, slot, at_k(dst))

        def begin(self):
            start(self.full(8, k, across))
            start(self.full(0, k, fore))
            start(self.full(1, k, back))

        def middle(self):
            self.full(8, across, across).wait_recv()
            start(self.full(2, across, fore))
            start(self.full(3, across, back))
            self.full(0, back, fore).wait_recv()
            start(self.part(4, back, fore))
            self.full(1, fore, back).wait_recv()
            start(self.part(5, fore, back))
            self.full(2, back_x, fore).wait_recv()
            start(self.part(6, back_x, fore))
            self.full(3, fore_x, back).wait_recv()
            start(self.part(7, fore_x, back))

        def late(self):
            return ((half, (4, 5)), (half_x, (6, 7)))

        def wait_late(self, src, slots):
            for slot in slots:
                self.part(slot, src, fore).wait_recv()

    green[...] = blocks_of_green(w_count, trial_ref, walkers_ref, first_window)

    def first_copy(d):
        dst = to_w(d)
        return remote(green.at[span(dst, SLOT)], first_buf.at[w], first_sems, d, at_w(dst))

    start_each(w_count, first_copy)
    first_buf[w] = green[span(w, SLOT), :]

    def aux_piece(which):
        shape = (per_w, aux_ref.shape[1])
        pick = jnp.where(iota(shape, 1) == walker_of(iota(shape, 0) + per_w * w, which), 1.0, 0.0)
        return dot(pick, aux_ref[...], ((1,), (1,)), HIGH)

    aux_out[...] = jnp.zeros_like(aux_out)
    aux_out[:, :vec_count] = aux_piece(other)
    start(aux_copy)
    aux_buf[core] = jnp.zeros(aux_buf.shape[1:], F32)
    aux_buf[core, :, :vec_count] = aux_piece(core)

    pick = permutation(
        each * per_k,
        w_count * SLOT,
        lambda r: lax.rem(r, per_k) // owned * SLOT + lax.rem(r, owned) * each + lax.div(r, per_k),
    )
    wide_f32[...] = jnp.zeros_like(wide_f32)
    each_of(w_count, lambda d: first_copy(d).wait_recv())
    picked = dot(pick, first_buf[...].reshape(w_count * SLOT, orbitals))
    for i in range(each):
        wide_f32[:, i * orbitals : (i + 1) * orbitals] = picked[i * per_k : (i + 1) * per_k, :]
    entries[k] = wide_f32[...].astype(BF16)
    gather = Gather(entries, entry_sems, per_k)
    gather.begin()
    hr_copy.wait_recv()
    gather.middle()
    for src, slots in gather.late():
        gather.wait_late(src, slots)
    partial[...] = dot(
        entries[...].reshape(rows, entries.shape[-1]), hr_buf[...].reshape(2 * gp, entries.shape[-1]), ((1,), (1,))
    )

    def partial_copy(d):
        dst = to_w(d)
        return remote(partial.at[span(dst, per_w)], partial_in.at[w], partial_sems, d, at_w(dst))

    start_each(w_count, partial_copy)
    second_window()
    partial_in[w] = partial[span(w, per_w), :]
    finish_first_window()
    aux_copy.wait_recv()
    aux = jnp.concatenate([aux_buf[0], aux_buf[1]], axis=1)
    each_of(w_count, lambda d: partial_copy(d).wait_recv())
    bias = jnp.sum(partial_in[...], axis=0)
    piece_b[...] = bias
    piece_f[...] = (aux - bias).astype(BF16)

    my_rows = span(w, per_w)

    def field_copy(d):
        return remote(piece_f, fields.at[k, my_rows], field_w_sems, d, at_w(to_w(d)))

    start_each(w_count, field_copy)
    fields[k, my_rows, :] = piece_f[...]

    def bias_copy(d):
        return remote(piece_b, bias_in.at[my_rows], bias_sems, d, at_w(to_w(d)))

    each_of(w_count, lambda d: field_copy(d).wait_recv())
    gather = Gather(fields, field_c_sems, rows)
    gather.begin()
    start_each(w_count, bias_copy)
    bias_in[my_rows, :] = piece_b[...]
    gather.middle()
    finish_second_window()

    def term(kk, columns):
        return dot(fields[kk], vecs_buf[kk, :, :, columns].reshape(2 * gp, part_width))

    def hop1(d, n):
        dst = to_k(d)
        return remote(out.at[n, span(dst, per_k)], one_in.at[n, k], hop1_sems, n * k_count + d, at_k(dst))

    def hop2(d, n):
        dst = to_w(d)
        return remote(two_out.at[n, span(dst, per_w)], result_ref.at[n, w], hop2_sems, n * w_count + d, at_w(dst))

    for n in range(CHUNKS):
        columns = slice(n * part_width, (n + 1) * part_width)
        total = None
        for kk in (k, across, back, fore, back_x, fore_x, half, half_x):
            if n == 0:
                vec_from_sibling(kk).wait_recv()
                for src, slots in gather.late():
                    if kk is src:
                        gather.wait_late(src, slots)
            total = term(kk, columns) if total is None else total + term(kk, columns)
        out[n] = total.astype(BF16)
        start_each(k_count, functools.partial(hop1, n=n))
        one_in[n, k] = out[n, span(k, per_k), :]

    regroup = permutation(rows, rows, lambda r: lax.rem(lax.div(r, owned), k_count) * per_k + lax.div(r, per_w) * owned + lax.rem(r, owned))
    for n in range(CHUNKS):
        each_of(k_count, lambda d: hop1(d, n).wait_recv())
        two_out[n] = dot(regroup, one_in[n].reshape(rows, part_width)).astype(BF16)
        start_each(w_count, functools.partial(hop2, n=n))
        result_ref[n, w] = two_out[n, span(w, per_w), :]

    each_of(w_count, lambda d: bias_copy(d).wait_recv())
    low, high = bias_in[:, :gp], bias_in[:, gp:]
    bias_out[...] = jnp.where(core == 0, high, low)
    sib_copy = start(remote(bias_out, bias_sib, one_sems, 2, sibling))

    def spread(which):
        shape = (rows, bias_ref.shape[1])
        return jnp.where(iota(shape, 1) == walker_of(iota(shape, 0), which), 1.0, 0.0)

    mine = dot(jnp.where(core == 0, low, high), spread(core), ((0,), (0,)), HIGH)
    sib_copy.wait_recv()
    theirs = dot(bias_sib[...], spread(other), ((0,), (0,)), HIGH)
    bias_ref[...] = (mine + theirs)[:vec_count]

    for n in range(CHUNKS):
        each_of(w_count, lambda d: hop2(d, n).wait_recv())
    for drain in drains:
        drain()


def taylor_kernel(k_count, walkers_ref, pieces_ref, out_ref, flat, stacked):
    owned, _, orbitals = walkers_ref.shape
    chunks, w_count, per_w, part_width = pieces_ref.shape
    width = chunks * part_width
    each = orbitals // w_count
    rows = w_count * per_w
    order = permutation(
        rows, rows, lambda r: lax.rem(r, w_count) * per_w + lax.rem(lax.div(r, w_count), k_count) * owned + lax.div(r, w_count * k_count)
    )
    sorted_ = [dot(order, pieces_ref[n].reshape(rows, part_width)) for n in range(chunks)]
    place = permutation(orbitals, orbitals, lambda r: lax.rem(r, each) * w_count + lax.div(r, each))
    terms, totals, onebody = [], [], []
    for j in range(owned):
        for kk in range(k_count):
            at = (j * k_count + kk) * w_count
            for n in range(chunks):
                lane = kk * width + n * part_width
                flat[j, :, lane : lane + part_width] = sorted_[n][at : at + w_count, :]
        for q in range(each):
            stacked[j, q * w_count : (q + 1) * w_count, :] = flat[j, :, q * orbitals : (q + 1) * orbitals].astype(BF16)
        onebody.append(dot(stacked[j], place, ((0,), (1,))).astype(BF16))
        terms.append(walkers_ref[j])
        totals.append(walkers_ref[j])
    for step in range(1, TAYLOR + 1):
        for j in range(owned):
            head = terms[j].astype(BF16)
            rest = (terms[j] - head.astype(F32)).astype(BF16)
            terms[j] = (dot(head, onebody[j]) + dot(rest, onebody[j])) * (-1.0 / step)
            totals[j] = totals[j] + terms[j]
    for j in range(owned):
        out_ref[j] = totals[j]


def body(trial, walkers, aux_field, half_rotated, cholesky_vecs):
    k_count = lax.axis_size("chol") // 2
    w_count = lax.axis_size("walk")
    assert k_count == SIDE * LINE
    owned, electrons, orbitals = walkers.shape
    vec_count, local_entries = half_rotated.shape
    walker_count = aux_field.shape[0]
    local_pairs = cholesky_vecs.shape[1]
    each = electrons // w_count
    gp = up(vec_count, 32)
    lanes = up(local_entries, 128)
    width = up(-(-local_pairs // k_count), 128 * CHUNKS)
    part_width = width // CHUNKS
    rows = k_count * w_count * owned
    per_k, per_w = w_count * owned, k_count * owned
    vmem = pl.BlockSpec(memory_space=pltpu.VMEM)
    dma = pltpu.SemaphoreType.DMA
    pieces, force_bias = pl.pallas_call(
        functools.partial(exchange_kernel, (k_count, w_count, owned, each, orbitals, vec_count)),
        out_shape=(
            jax.ShapeDtypeStruct((CHUNKS, w_count, per_w, part_width), BF16),
            jax.ShapeDtypeStruct((vec_count, walker_count), F32),
        ),
        in_specs=[vmem] * 5,
        out_specs=(vmem, vmem),
        scratch_shapes=[
            pltpu.VMEM((w_count * SLOT, orbitals), BF16),
            pltpu.VMEM((2, gp, lanes), BF16),
            pltpu.VMEM((per_w, gp), F32),
            pltpu.VMEM((2, per_w, gp), F32),
            pltpu.VMEM((gp, k_count * width), BF16),
            pltpu.VMEM((k_count, 2, gp, width), BF16),
            pltpu.VMEM((2, gp // 2, width), BF16),
            pltpu.VMEM((w_count, SLOT, orbitals), BF16),
            pltpu.VMEM((per_k, lanes), F32),
            pltpu.VMEM((k_count, per_k, lanes), BF16),
            pltpu.VMEM((rows, 2 * gp), F32),
            pltpu.VMEM((w_count, per_w, 2 * gp), F32),
            pltpu.VMEM((per_w, 2 * gp), BF16),
            pltpu.VMEM((per_w, 2 * gp), F32),
            pltpu.VMEM((k_count, rows, 2 * gp), BF16),
            pltpu.VMEM((rows, 2 * gp), F32),
            pltpu.VMEM((rows, gp), F32),
            pltpu.VMEM((rows, gp), F32),
            pltpu.VMEM((CHUNKS, rows, part_width), BF16),
            pltpu.VMEM((CHUNKS, k_count, per_k, part_width), BF16),
            pltpu.VMEM((CHUNKS, rows, part_width), BF16),
            dma((3, 3)),
            dma((2, 11)),
            dma((2, k_count)),
            dma((2, w_count)),
            dma((2, 9)),
            dma((2, w_count)),
            dma((2, w_count)),
            dma((2, 9)),
            dma((2, w_count)),
            dma((2, CHUNKS * k_count)),
            dma((2, CHUNKS * w_count)),
        ],
        compiler_params=pltpu.CompilerParams(collective_id=0, has_side_effects=True, vmem_limit_bytes=48 * 1024 * 1024),
    )(trial, walkers, half_rotated, aux_field.T, cholesky_vecs)

    next_walkers = pl.pallas_call(
        functools.partial(taylor_kernel, k_count),
        out_shape=jax.ShapeDtypeStruct(walkers.shape, F32),
        in_specs=[vmem, vmem],
        out_specs=vmem,
        scratch_shapes=[
            pltpu.VMEM((owned, w_count, k_count * width), F32),
            pltpu.VMEM((owned, orbitals, orbitals), BF16),
        ],
        compiler_params=pltpu.CompilerParams(vmem_limit_bytes=32 * 1024 * 1024),
    )(walkers, pieces)
    return (next_walkers, force_bias.T)


def solution(mesh):
    in_specs = (
        P(),
        P(("chol", "walk"), None, None),
        P(None, "chol"),
        P("chol", "walk"),
        P("chol", "walk"),
    )
    out_specs = (P(("chol", "walk"), None, None), P(None, "chol"))
    return jax.shard_map(body, mesh=mesh, in_specs=in_specs, out_specs=out_specs, check_vma=False)
```

```python
import functools

import jax
import jax.numpy as jnp
from jax import lax
from jax.experimental import pallas as pl
from jax.experimental.pallas import tpu as pltpu
from jax.sharding import PartitionSpec as P

TAYLOR = 6
SIDE, LINE = 2, 4
CHUNKS = 2
LAG = 1
HIGH = lax.Precision.HIGHEST
MESH = pl.DeviceIdType.MESH
F32 = jnp.float32
BF16 = jnp.bfloat16
SLOT = 16


def up(value, multiple):
    return -(-value // multiple) * multiple


def iota(shape, dim):
    return lax.broadcasted_iota(jnp.int32, shape, dim)


def permutation(rows, cols, source):
    return jnp.where(iota((rows, cols), 1) == source(iota((rows, cols), 0)), 1.0, 0.0).astype(BF16)


def dot(a, b, contract=((1,), (0,)), precision=None):
    return lax.dot_general(a, b, (contract, ((), ())), preferred_element_type=F32, precision=precision)


def invert(grams):
    size = grams[0].shape[0]
    rows = iota((size, size), 0)
    lanes = iota((1, size), 1)

    def pair(a, k):
        one = jnp.broadcast_to(a[:, k : k + 1], (size, size))
        two = jnp.broadcast_to(a[:, k + 1 : k + 2], (size, size))
        e11, e21, e12, e22 = one[k : k + 1], one[k + 1 : k + 2], two[k : k + 1], two[k + 1 : k + 2]
        first = 1.0 / e11
        right, below = first * e12, e21 * first
        p22 = 1.0 / (e22 - below * e12)
        p12, p21 = -right * p22, -p22 * below
        p11 = first + right * p22 * below
        upper = jnp.where(lanes == k, 1.0, jnp.where(lanes == k + 1, 0.0, a[k : k + 1]))
        lower = jnp.where(lanes == k, 0.0, jnp.where(lanes == k + 1, 1.0, a[k + 1 : k + 2]))
        upper, lower = p11 * upper + p12 * lower, p21 * upper + p22 * lower
        kept = jnp.where((lanes == k) | (lanes == k + 1), 0.0, a)
        return jnp.where(rows == k, upper, jnp.where(rows == k + 1, lower, kept - one * upper - two * lower))

    for k in range(0, size, 2):
        grams = [pair(a, k) for a in grams]
    return grams


def blocks_of_green(parts, trial_ref, walkers_ref, before_inverse):
    count, electrons, _ = walkers_ref.shape
    each = electrons // parts
    trial = trial_ref[...]
    walkers = [walkers_ref[j] for j in range(count)]
    corr = [dot(trial, w, ((1,), (1,)), HIGH) for w in walkers]
    grams = [dot(c, c, ((1,), (1,)), HIGH) for c in corr]
    before_inverse()
    rhs = [dot(c, w, precision=HIGH) for c, w in zip(corr, walkers)]
    inverse = invert(grams)
    green = [dot(g, r, precision=HIGH).astype(BF16) for g, r in zip(inverse, rhs)]
    total = None
    for j in range(count):

        def source(r):
            inside = r % SLOT - each * j
            return jnp.where((inside >= 0) & (inside < each), (r // SLOT) * each + inside, -1)

        part = dot(permutation(parts * SLOT, electrons, source), green[j])
        total = part if total is None else total + part
    return total.astype(BF16)


def exchange_kernel(
    dims,
    trial_hbm,
    walkers_hbm,
    hr_ref,
    aux_hbm,
    vecs_ref,
    result_ref,
    bias_ref,
    trial_ref,
    walkers_ref,
    aux_ref,
    green,
    hr_buf,
    aux_out,
    aux_buf,
    vecs_out,
    vecs_buf,
    relay,
    first_buf,
    wide_f32,
    entries,
    partial,
    partial_in,
    piece_f,
    piece_b,
    fields,
    bias_in,
    bias_out,
    bias_sib,
    out,
    one_in,
    two_out,
    load_sems,
    one_sems,
    vec_sems,
    fwd_sems,
    first_sems,
    entry_sems,
    partial_sems,
    field_w_sems,
    field_c_sems,
    bias_sems,
    hop1_sems,
    hop2_sems,
):
    k_count, w_count, owned, each, orbitals, vec_count = dims
    c = lax.axis_index("chol")
    w = lax.axis_index("walk")
    core = lax.rem(c, 2)
    k = lax.div(c, 2)
    other = 1 - core
    sibling = (2 * k + other, w)
    gp = hr_buf.shape[1]
    width = vecs_buf.shape[-1]
    part_width = width // CHUNKS
    rows = k_count * w_count * owned
    per_k = w_count * owned
    per_w = k_count * owned
    local_pairs = vecs_ref.shape[1]
    local_entries = hr_ref.shape[1]

    line = LINE * lax.div(k, LINE)
    across = lax.rem(k + LINE, k_count)
    line_across = lax.rem(line + LINE, k_count)

    def along(start, step):
        return start + lax.rem(k - line + step, LINE)

    fore, back, half = along(line, 1), along(line, LINE - 1), along(line, 2)
    fore_x, back_x, half_x = along(line_across, 1), along(line_across, LINE - 1), along(line_across, 2)

    def at_k(kk):
        return (2 * kk + core, w)

    def at_w(ww):
        return (c, ww)

    ring = w_count // SIDE
    side = lax.div(w, ring)

    def at_near(ww):
        return (2 * jnp.where(lax.div(ww, ring) == side, k, across) + core, ww)

    def block(piece, on_side):
        kk = lax.div(piece, SIDE)
        return SIDE * jnp.where(lax.rem(piece, SIDE) == on_side, kk, lax.rem(kk + LINE, k_count)) + lax.rem(piece, SIDE)

    def remote(src, dst, sems, slot, device):
        return pltpu.make_async_remote_copy(
            src_ref=src, dst_ref=dst, send_sem=sems.at[0, slot], recv_sem=sems.at[1, slot], device_id=device, device_id_type=MESH
        )

    drains = []

    def start(copy):
        copy.start()
        drains.append(copy.wait_send)
        return copy

    def each_of(count, body, first=1):
        def step(d, carry):
            body(d)
            return carry

        lax.fori_loop(first, count, step, 0)

    def start_each(count, make):
        each_of(count, lambda d: make(d).start())
        drains.append(lambda: each_of(count, lambda d: make(d).wait_send()))

    def to_k(d):
        return lax.rem(k + d, k_count)

    def to_w(d):
        return lax.rem(w + d, w_count)

    def walker_of(row, which):
        return per_k * (2 * lax.div(row, per_k) + which) + lax.rem(row, per_k)

    def span(index, size):
        return pl.ds(pl.multiple_of(index * size, size), size)

    pairs = ((trial_hbm, trial_ref), (walkers_hbm, walkers_ref), (aux_hbm, aux_ref))
    load_trial, load_walkers, load_aux = loads = [
        pltpu.make_async_copy(src, dst, load_sems.at[n]) for n, (src, dst) in enumerate(pairs)
    ]
    for load in loads:
        load.start()

    barrier = pltpu.get_barrier_semaphore()
    each_of(k_count, lambda d: pl.semaphore_signal(barrier, inc=1, device_id=at_k(to_k(d)), device_id_type=MESH))
    each_of(w_count, lambda d: pl.semaphore_signal(barrier, inc=1, device_id=at_w(to_w(d)), device_id_type=MESH))
    opposite = ring * (SIDE - 1 - side)
    each_of(ring, lambda d: pl.semaphore_signal(barrier, inc=1, device_id=at_near(opposite + d), device_id_type=MESH), 0)
    pl.semaphore_signal(barrier, inc=1, device_id=sibling, device_id_type=MESH)

    def pad_vectors():
        edge = local_pairs // 128 * 128
        vecs_out[gp - 16 :, :] = jnp.zeros((16, vecs_out.shape[1]), BF16)
        if edge < vecs_out.shape[1]:
            vecs_out[:, edge:] = jnp.zeros((gp, vecs_out.shape[1] - edge), BF16)
        vecs_out[:vec_count, :local_pairs] = vecs_ref[...]
        hr_buf[core] = jnp.zeros(hr_buf.shape[1:], BF16)
        hr_buf[core, :vec_count, :local_entries] = hr_ref[...]

    cut = gp // 2
    lower, upper = pl.ds(0, cut), pl.ds(cut, gp - cut)

    def vec_full(slot, dst, src):
        return remote(vecs_out.at[:, span(dst, width)], vecs_buf.at[src, core], vec_sems, slot, at_k(dst))

    def vec_lower(slot, dst, src):
        return remote(vecs_out.at[lower, span(dst, width)], vecs_buf.at[src, core, lower], vec_sems, slot, at_k(dst))

    def vec_relay(slot, dst, by):
        return remote(vecs_out.at[upper, span(dst, width)], relay.at[slot - 7], vec_sems, slot, at_k(by))

    def vec_upper(slot, dst, src):
        return remote(relay.at[slot - 9], vecs_buf.at[src, core, upper], vec_sems, slot, at_k(dst))

    def vec_forward(kk):
        return remote(vecs_buf.at[kk, core], vecs_buf.at[kk, core], fwd_sems, kk, sibling)

    def vec_from_sibling(kk):
        return remote(vecs_buf.at[kk, other], vecs_buf.at[kk, other], fwd_sems, kk, sibling)

    own_vecs = pltpu.make_async_copy(vecs_out.at[:, span(k, width)], vecs_buf.at[k, core], one_sems.at[2, 0])
    hr_copy = remote(hr_buf.at[core], hr_buf.at[core], one_sems, 0, sibling)
    aux_copy = remote(aux_out, aux_buf.at[core], one_sems, 1, sibling)

    def first_window():
        pad_vectors()
        pl.semaphore_wait(barrier, k_count + w_count - 1 + ring)
        start(vec_relay(7, half, back))
        start(vec_relay(8, half_x, back))
        start(vec_full(0, fore, k))
        start(vec_full(1, back, k))
        start(vec_full(3, fore_x, k))
        start(vec_full(4, back_x, k))
        own_vecs.start()
        start(hr_copy)

    def second_window():
        start(vec_full(2, across, k))

    def third_window():
        start(vec_lower(5, half, k))
        start(vec_lower(6, half_x, k))
        vec_relay(7, half, back).wait_recv()
        start(vec_upper(9, back, fore))
        vec_relay(8, half_x, back).wait_recv()
        start(vec_upper(10, back_x, fore))

    def finish_first_window():
        own_vecs.wait()
        start(vec_forward(k))
        for slot, src in ((0, back), (1, fore), (3, back_x), (4, fore_x)):
            vec_full(slot, k, src).wait_recv()
            start(vec_forward(src))

    def finish_others():
        vec_full(2, k, across).wait_recv()
        start(vec_forward(across))
        for slots, src in (((5, 9), half), ((6, 10), half_x)):
            vec_lower(slots[0], k, src).wait_recv()
            vec_upper(slots[1], k, src).wait_recv()
            start(vec_forward(src))

    class Gather:
        def __init__(self, buf, sems, size):
            self.buf, self.sems = buf, sems
            self.halves = pl.ds(0, size // 2), pl.ds(size // 2, size - size // 2)

        def full(self, slot, src, dst):
            return remote(self.buf.at[src], self.buf.at[src], self.sems, slot, at_k(dst))

        def part(self, slot, src, dst):
            ref = self.buf.at[src, self.halves[slot % 2]]
            return remote(ref, ref, self.sems, slot, at_k(dst))

        def begin(self):
            start(self.full(8, k, across))
            start(self.full(0, k, fore))
            start(self.full(1, k, back))

        def middle(self, then=lambda: None):
            self.full(8, across, across).wait_recv()
            start(self.full(2, across, fore))
            start(self.full(3, across, back))
            then()
            self.full(0, back, fore).wait_recv()
            start(self.part(4, back, fore))
            self.full(1, fore, back).wait_recv()
            start(self.part(5, fore, back))
            self.full(2, back_x, fore).wait_recv()
            start(self.part(6, back_x, fore))
            self.full(3, fore_x, back).wait_recv()
            start(self.part(7, fore_x, back))

        def late(self):
            return ((half, (4, 5)), (half_x, (6, 7)))

        def wait_late(self, src, slots):
            for slot in slots:
                self.part(slot, src, fore).wait_recv()

    load_trial.wait()
    load_walkers.wait()
    green[...] = blocks_of_green(w_count, trial_ref, walkers_ref, first_window)

    def first_copy(d):
        dst = to_w(d)
        return remote(green.at[span(dst, SLOT)], first_buf.at[w], first_sems, d, at_near(dst))

    start_each(w_count, first_copy)
    first_buf[w] = green[span(w, SLOT), :]

    def aux_piece(which):
        shape = (per_w, aux_ref.shape[1])
        pick = jnp.where(iota(shape, 1) == walker_of(iota(shape, 0) + per_w * w, which), 1.0, 0.0)
        return dot(pick, aux_ref[...], ((1,), (1,)), HIGH)

    load_aux.wait()
    aux_out[...] = jnp.zeros_like(aux_out)
    aux_out[:, :vec_count] = aux_piece(other)
    start(aux_copy)
    aux_buf[core] = jnp.zeros(aux_buf.shape[1:], F32)
    aux_buf[core, :, :vec_count] = aux_piece(core)

    pick = permutation(
        each * per_k,
        w_count * SLOT,
        lambda r: lax.rem(r, per_k) // owned * SLOT + lax.rem(r, owned) * each + lax.div(r, per_k),
    )
    wide_f32[...] = jnp.zeros_like(wide_f32)
    each_of(w_count, lambda d: first_copy(d).wait_recv())
    picked = dot(pick, first_buf[...].reshape(w_count * SLOT, orbitals))
    for i in range(each):
        wide_f32[:, i * orbitals : (i + 1) * orbitals] = picked[i * per_k : (i + 1) * per_k, :]
    entries[k] = wide_f32[...].astype(BF16)
    gather = Gather(entries, entry_sems, per_k)
    gather.begin()
    hr_copy.wait_recv()
    gather.middle(second_window)
    for src, slots in gather.late():
        gather.wait_late(src, slots)
    partial[...] = dot(
        entries[...].reshape(rows, entries.shape[-1]), hr_buf[...].reshape(2 * gp, entries.shape[-1]), ((1,), (1,))
    )

    def partial_copy(d):
        dst = to_w(d)
        return remote(partial.at[span(block(dst, side), per_w)], partial_in.at[w], partial_sems, d, at_w(dst))

    start_each(w_count, partial_copy)
    third_window()
    partial_in[w] = partial[span(block(w, side), per_w), :]
    finish_first_window()
    aux_copy.wait_recv()
    aux = jnp.concatenate([aux_buf[0], aux_buf[1]], axis=1)
    each_of(w_count, lambda d: partial_copy(d).wait_recv())
    bias = jnp.sum(partial_in[...], axis=0)
    piece_b[...] = bias
    piece_f[...] = (aux - bias).astype(BF16)

    my_rows = span(w, per_w)

    def field_copy(d):
        dst = to_w(d)
        return remote(piece_f, fields.at[k, span(block(w, lax.div(dst, ring)), per_w)], field_w_sems, d, at_w(dst))

    start_each(w_count, field_copy)
    fields[k, span(block(w, side), per_w), :] = piece_f[...]

    def bias_copy(d):
        return remote(piece_b, bias_in.at[my_rows], bias_sems, d, at_w(to_w(d)))

    each_of(w_count, lambda d: field_copy(d).wait_recv())
    gather = Gather(fields, field_c_sems, rows)
    gather.begin()
    bias_in[my_rows, :] = piece_b[...]
    start_each(w_count, bias_copy)
    gather.middle()
    finish_others()

    def term(kk, columns):
        return dot(fields[kk], vecs_buf[kk, :, :, columns].reshape(2 * gp, part_width))

    def hop1(d, n):
        dst = to_k(d)
        return remote(out.at[n, span(dst, per_k)], one_in.at[n, k], hop1_sems, n * k_count + d, at_k(dst))

    def hop2(d, n):
        dst = to_w(d)
        return remote(two_out.at[n, span(dst, per_w)], result_ref.at[n, w], hop2_sems, n * w_count + d, at_near(dst))

    regroup = permutation(rows, rows, lambda r: lax.rem(lax.div(r, owned), k_count) * per_k + lax.div(r, per_w) * owned + lax.rem(r, owned))

    for step in range(CHUNKS + LAG):
        n = step
        if n < CHUNKS:
            columns = slice(n * part_width, (n + 1) * part_width)
            total = None
            for kk in (k, back, fore, back_x, fore_x, across, half, half_x):
                if n == 0:
                    vec_from_sibling(kk).wait_recv()
                    for src, slots in gather.late():
                        if kk is src:
                            gather.wait_late(src, slots)
                total = term(kk, columns) if total is None else total + term(kk, columns)
            out[n] = total.astype(BF16)
            start_each(k_count, functools.partial(hop1, n=n))
            one_in[n, k] = out[n, span(k, per_k), :]
        n = step - LAG
        if n >= 0:
            each_of(k_count, lambda d: hop1(d, n).wait_recv())
            two_out[n] = dot(regroup, one_in[n].reshape(rows, part_width)).astype(BF16)
            start_each(w_count, functools.partial(hop2, n=n))
            result_ref[n, w] = two_out[n, span(w, per_w), :]

    each_of(w_count, lambda d: bias_copy(d).wait_recv())
    low, high = bias_in[:, :gp], bias_in[:, gp:]
    bias_out[...] = jnp.where(core == 0, high, low)
    sib_copy = start(remote(bias_out, bias_sib, one_sems, 2, sibling))

    def spread(which):
        shape = (rows, bias_ref.shape[1])
        return jnp.where(iota(shape, 1) == walker_of(iota(shape, 0), which), 1.0, 0.0)

    mine = dot(jnp.where(core == 0, low, high), spread(core), ((0,), (0,)), HIGH)
    sib_copy.wait_recv()
    theirs = dot(bias_sib[...], spread(other), ((0,), (0,)), HIGH)
    bias_ref[...] = (mine + theirs)[:vec_count]

    for n in range(CHUNKS):
        each_of(w_count, lambda d: hop2(d, n).wait_recv())
    for drain in drains:
        drain()


def taylor_kernel(k_count, walkers_ref, pieces_ref, bias_ref, out_ref, bias_out, flat, stacked):
    bias_out[...] = bias_ref[...]
    owned, _, orbitals = walkers_ref.shape
    chunks, w_count, per_w, part_width = pieces_ref.shape
    width = chunks * part_width
    each = orbitals // w_count
    rows = w_count * per_w
    order = permutation(
        rows, rows, lambda r: lax.rem(r, w_count) * per_w + lax.rem(lax.div(r, w_count), k_count) * owned + lax.div(r, w_count * k_count)
    )
    sorted_ = [dot(order, pieces_ref[n].reshape(rows, part_width)) for n in range(chunks)]
    place = permutation(orbitals, orbitals, lambda r: lax.rem(r, each) * w_count + lax.div(r, each))
    terms, totals, onebody = [], [], []
    for j in range(owned):
        for kk in range(k_count):
            at = (j * k_count + kk) * w_count
            for n in range(chunks):
                lane = kk * width + n * part_width
                flat[j, :, lane : lane + part_width] = sorted_[n][at : at + w_count, :]
        for q in range(each):
            stacked[j, q * w_count : (q + 1) * w_count, :] = flat[j, :, q * orbitals : (q + 1) * orbitals].astype(BF16)
        onebody.append(dot(stacked[j], place, ((0,), (1,))).astype(BF16))
        terms.append(walkers_ref[j])
        totals.append(walkers_ref[j])
    for step in range(1, TAYLOR + 1):
        for j in range(owned):
            head = terms[j].astype(BF16)
            rest = (terms[j] - head.astype(F32)).astype(BF16)
            terms[j] = (dot(head, onebody[j]) + dot(rest, onebody[j])) * (-1.0 / step)
            totals[j] = totals[j] + terms[j]
    for j in range(owned):
        out_ref[j] = totals[j]


def body(trial, walkers, aux_field, half_rotated, cholesky_vecs):
    k_count = lax.axis_size("chol") // 2
    w_count = lax.axis_size("walk")
    assert k_count == SIDE * LINE and w_count == SIDE * k_count
    owned, electrons, orbitals = walkers.shape
    vec_count, local_entries = half_rotated.shape
    walker_count = aux_field.shape[0]
    local_pairs = cholesky_vecs.shape[1]
    each = electrons // w_count
    gp = up(vec_count, 32)
    lanes = up(local_entries, 128)
    width = up(-(-local_pairs // k_count), 128 * CHUNKS)
    part_width = width // CHUNKS
    rows = k_count * w_count * owned
    per_k, per_w = w_count * owned, k_count * owned
    vmem = pl.BlockSpec(memory_space=pltpu.VMEM)
    hbm = pl.BlockSpec(memory_space=pltpu.HBM)
    dma = pltpu.SemaphoreType.DMA
    pieces, force_bias = pl.pallas_call(
        functools.partial(exchange_kernel, (k_count, w_count, owned, each, orbitals, vec_count)),
        out_shape=(
            jax.ShapeDtypeStruct((CHUNKS, w_count, per_w, part_width), BF16),
            jax.ShapeDtypeStruct((vec_count, walker_count), F32),
        ),
        in_specs=[hbm, hbm, vmem, hbm, vmem],
        out_specs=(vmem, vmem),
        scratch_shapes=[
            pltpu.VMEM(trial.shape, F32),
            pltpu.VMEM(walkers.shape, F32),
            pltpu.VMEM((vec_count, walker_count), F32),
            pltpu.VMEM((w_count * SLOT, orbitals), BF16),
            pltpu.VMEM((2, gp, lanes), BF16),
            pltpu.VMEM((per_w, gp), F32),
            pltpu.VMEM((2, per_w, gp), F32),
            pltpu.VMEM((gp, k_count * width), BF16),
            pltpu.VMEM((k_count, 2, gp, width), BF16),
            pltpu.VMEM((2, gp // 2, width), BF16),
            pltpu.VMEM((w_count, SLOT, orbitals), BF16),
            pltpu.VMEM((per_k, lanes), F32),
            pltpu.VMEM((k_count, per_k, lanes), BF16),
            pltpu.VMEM((rows, 2 * gp), F32),
            pltpu.VMEM((w_count, per_w, 2 * gp), F32),
            pltpu.VMEM((per_w, 2 * gp), BF16),
            pltpu.VMEM((per_w, 2 * gp), F32),
            pltpu.VMEM((k_count, rows, 2 * gp), BF16),
            pltpu.VMEM((rows, 2 * gp), F32),
            pltpu.VMEM((rows, gp), F32),
            pltpu.VMEM((rows, gp), F32),
            pltpu.VMEM((CHUNKS, rows, part_width), BF16),
            pltpu.VMEM((CHUNKS, k_count, per_k, part_width), BF16),
            pltpu.VMEM((CHUNKS, rows, part_width), BF16),
            dma((3,)),
            dma((3, 3)),
            dma((2, 11)),
            dma((2, k_count)),
            dma((2, w_count)),
            dma((2, 9)),
            dma((2, w_count)),
            dma((2, w_count)),
            dma((2, 9)),
            dma((2, w_count)),
            dma((2, CHUNKS * k_count)),
            dma((2, CHUNKS * w_count)),
        ],
        compiler_params=pltpu.CompilerParams(collective_id=0, has_side_effects=True, vmem_limit_bytes=48 * 1024 * 1024),
    )(trial, walkers, half_rotated, aux_field.T, cholesky_vecs)

    next_walkers, force_bias = pl.pallas_call(
        functools.partial(taylor_kernel, k_count),
        out_shape=(jax.ShapeDtypeStruct(walkers.shape, F32), jax.ShapeDtypeStruct(force_bias.shape, F32)),
        in_specs=[vmem, vmem, vmem],
        out_specs=(vmem, vmem),
        scratch_shapes=[
            pltpu.VMEM((owned, w_count, k_count * width), F32),
            pltpu.VMEM((owned, orbitals, orbitals), BF16),
        ],
        compiler_params=pltpu.CompilerParams(vmem_limit_bytes=32 * 1024 * 1024),
    )(walkers, pieces, force_bias)
    return (next_walkers, force_bias.T)


def solution(mesh):
    in_specs = (
        P(),
        P(("chol", "walk"), None, None),
        P(None, "chol"),
        P("chol", "walk"),
        P("chol", "walk"),
    )
    out_specs = (P(("chol", "walk"), None, None), P(None, "chol"))
    return jax.shard_map(body, mesh=mesh, in_specs=in_specs, out_specs=out_specs, check_vma=False)
```

```python
import functools

import jax
import jax.numpy as jnp
from jax import lax
from jax.experimental import pallas as pl
from jax.experimental.pallas import tpu as pltpu
from jax.sharding import PartitionSpec as P

TAYLOR = 6
SIDE, LINE = 2, 4
CHUNKS = 2
LAG = 1
HIGH = lax.Precision.HIGHEST
MESH = pl.DeviceIdType.MESH
F32 = jnp.float32
BF16 = jnp.bfloat16
VMEM_BYTES = 62 * 1024 * 1024
SLOT = 16


def up(value, multiple):
    return -(-value // multiple) * multiple


def iota(shape, dim):
    return lax.broadcasted_iota(jnp.int32, shape, dim)


def permutation(rows, cols, source):
    return jnp.where(iota((rows, cols), 1) == source(iota((rows, cols), 0)), 1.0, 0.0).astype(BF16)


def dot(a, b, contract=((1,), (0,)), precision=None):
    return lax.dot_general(a, b, (contract, ((), ())), preferred_element_type=F32, precision=precision)


def invert(grams):
    size = grams[0].shape[0]
    rows = iota((size, size), 0)
    lanes = iota((1, size), 1)

    def pair(a, k):
        one = jnp.broadcast_to(a[:, k : k + 1], (size, size))
        two = jnp.broadcast_to(a[:, k + 1 : k + 2], (size, size))
        e11, e21, e12, e22 = one[k : k + 1], one[k + 1 : k + 2], two[k : k + 1], two[k + 1 : k + 2]
        first = 1.0 / e11
        right, below = first * e12, e21 * first
        p22 = 1.0 / (e22 - below * e12)
        p12, p21 = -right * p22, -p22 * below
        p11 = first + right * p22 * below
        upper = jnp.where(lanes == k, 1.0, jnp.where(lanes == k + 1, 0.0, a[k : k + 1]))
        lower = jnp.where(lanes == k, 0.0, jnp.where(lanes == k + 1, 1.0, a[k + 1 : k + 2]))
        upper, lower = p11 * upper + p12 * lower, p21 * upper + p22 * lower
        kept = jnp.where((lanes == k) | (lanes == k + 1), 0.0, a)
        return jnp.where(rows == k, upper, jnp.where(rows == k + 1, lower, kept - one * upper - two * lower))

    for k in range(0, size, 2):
        grams = [pair(a, k) for a in grams]
    return grams


def blocks_of_green(parts, trial_ref, walkers_ref, before_inverse):
    count, electrons, _ = walkers_ref.shape
    each = electrons // parts
    trial = trial_ref[...]
    walkers = [walkers_ref[j] for j in range(count)]
    corr = [dot(trial, w, ((1,), (1,)), HIGH) for w in walkers]
    grams = [dot(c, c, ((1,), (1,)), HIGH) for c in corr]
    before_inverse()
    rhs = [dot(c, w, precision=HIGH) for c, w in zip(corr, walkers)]
    inverse = invert(grams)
    green = [dot(g, r, precision=HIGH).astype(BF16) for g, r in zip(inverse, rhs)]
    total = None
    for j in range(count):

        def source(r):
            inside = r % SLOT - each * j
            return jnp.where((inside >= 0) & (inside < each), (r // SLOT) * each + inside, -1)

        part = dot(permutation(parts * SLOT, electrons, source), green[j])
        total = part if total is None else total + part
    return total.astype(BF16)


def exchange_kernel(
    dims,
    trial_hbm,
    walkers_hbm,
    hr_hbm,
    aux_hbm,
    vecs_hbm,
    result_ref,
    bias_hbm,
    trial_ref,
    walkers_ref,
    aux_ref,
    vecs_ref,
    hr_ref,
    bias_ref,
    green,
    hr_buf,
    aux_out,
    aux_buf,
    vecs_out,
    vecs_buf,
    relay,
    first_buf,
    wide_f32,
    entries,
    partial,
    partial_in,
    piece_f,
    piece_b,
    fields,
    bias_in,
    bias_out,
    bias_sib,
    out,
    one_in,
    two_out,
    load_sems,
    one_sems,
    vec_sems,
    fwd_sems,
    first_sems,
    entry_sems,
    partial_sems,
    field_w_sems,
    field_c_sems,
    bias_sems,
    hop1_sems,
    hop2_sems,
):
    k_count, w_count, owned, each, orbitals, vec_count = dims
    c = lax.axis_index("chol")
    w = lax.axis_index("walk")
    core = lax.rem(c, 2)
    k = lax.div(c, 2)
    other = 1 - core
    sibling = (2 * k + other, w)
    gp = hr_buf.shape[1]
    width = vecs_buf.shape[-1]
    part_width = width // CHUNKS
    rows = k_count * w_count * owned
    per_k = w_count * owned
    per_w = k_count * owned
    local_pairs = vecs_ref.shape[1]
    local_entries = hr_ref.shape[1]

    line = LINE * lax.div(k, LINE)
    across = lax.rem(k + LINE, k_count)
    line_across = lax.rem(line + LINE, k_count)

    def along(start, step):
        return start + lax.rem(k - line + step, LINE)

    fore, back, half = along(line, 1), along(line, LINE - 1), along(line, 2)
    fore_x, back_x, half_x = along(line_across, 1), along(line_across, LINE - 1), along(line_across, 2)

    def at_k(kk):
        return (2 * kk + core, w)

    def at_w(ww):
        return (c, ww)

    ring = w_count // SIDE
    side = lax.div(w, ring)

    def at_near(ww):
        return (2 * jnp.where(lax.div(ww, ring) == side, k, across) + core, ww)

    def block(piece, on_side):
        kk = lax.div(piece, SIDE)
        return SIDE * jnp.where(lax.rem(piece, SIDE) == on_side, kk, lax.rem(kk + LINE, k_count)) + lax.rem(piece, SIDE)

    def remote(src, dst, sems, slot, device):
        return pltpu.make_async_remote_copy(
            src_ref=src, dst_ref=dst, send_sem=sems.at[0, slot], recv_sem=sems.at[1, slot], device_id=device, device_id_type=MESH
        )

    drains = []

    def start(copy):
        copy.start()
        drains.append(copy.wait_send)
        return copy

    def each_of(count, body, first=1):
        def step(d, carry):
            body(d)
            return carry

        lax.fori_loop(first, count, step, 0)

    def start_each(count, make):
        each_of(count, lambda d: make(d).start())
        drains.append(lambda: each_of(count, lambda d: make(d).wait_send()))

    def to_k(d):
        return lax.rem(k + d, k_count)

    def to_w(d):
        return lax.rem(w + d, w_count)

    def walker_of(row, which):
        return per_k * (2 * lax.div(row, per_k) + which) + lax.rem(row, per_k)

    def span(index, size):
        return pl.ds(pl.multiple_of(index * size, size), size)

    pairs = ((trial_hbm, trial_ref), (walkers_hbm, walkers_ref), (aux_hbm, aux_ref), (vecs_hbm, vecs_ref), (hr_hbm, hr_ref))
    load_trial, load_walkers, load_aux, load_vecs, load_hr = loads = [
        pltpu.make_async_copy(src, dst, load_sems.at[n]) for n, (src, dst) in enumerate(pairs)
    ]
    for load in loads:
        load.start()

    barrier = pltpu.get_barrier_semaphore()
    each_of(k_count, lambda d: pl.semaphore_signal(barrier, inc=1, device_id=at_k(to_k(d)), device_id_type=MESH))
    each_of(w_count, lambda d: pl.semaphore_signal(barrier, inc=1, device_id=at_w(to_w(d)), device_id_type=MESH))
    opposite = ring * (SIDE - 1 - side)
    each_of(ring, lambda d: pl.semaphore_signal(barrier, inc=1, device_id=at_near(opposite + d), device_id_type=MESH), 0)
    pl.semaphore_signal(barrier, inc=1, device_id=sibling, device_id_type=MESH)

    def pad_vectors():
        edge = local_pairs // 128 * 128
        vecs_out[gp - 16 :, :] = jnp.zeros((16, vecs_out.shape[1]), BF16)
        if edge < vecs_out.shape[1]:
            vecs_out[:, edge:] = jnp.zeros((gp, vecs_out.shape[1] - edge), BF16)
        load_vecs.wait()
        vecs_out[:vec_count, :local_pairs] = vecs_ref[...]
        hr_buf[core] = jnp.zeros(hr_buf.shape[1:], BF16)
        load_hr.wait()
        hr_buf[core, :vec_count, :local_entries] = hr_ref[...]

    cut = gp // 2
    lower, upper = pl.ds(0, cut), pl.ds(cut, gp - cut)

    def vec_full(slot, dst, src):
        return remote(vecs_out.at[:, span(dst, width)], vecs_buf.at[src, core], vec_sems, slot, at_k(dst))

    def vec_lower(slot, dst, src):
        return remote(vecs_out.at[lower, span(dst, width)], vecs_buf.at[src, core, lower], vec_sems, slot, at_k(dst))

    def vec_relay(slot, dst, by):
        return remote(vecs_out.at[upper, span(dst, width)], relay.at[slot - 7], vec_sems, slot, at_k(by))

    def vec_upper(slot, dst, src):
        return remote(relay.at[slot - 9], vecs_buf.at[src, core, upper], vec_sems, slot, at_k(dst))

    def vec_forward(kk):
        return remote(vecs_buf.at[kk, core], vecs_buf.at[kk, core], fwd_sems, kk, sibling)

    def vec_from_sibling(kk):
        return remote(vecs_buf.at[kk, other], vecs_buf.at[kk, other], fwd_sems, kk, sibling)

    own_vecs = pltpu.make_async_copy(vecs_out.at[:, span(k, width)], vecs_buf.at[k, core], one_sems.at[2, 0])
    hr_copy = remote(hr_buf.at[core], hr_buf.at[core], one_sems, 0, sibling)
    aux_copy = remote(aux_out, aux_buf.at[core], one_sems, 1, sibling)

    def first_window():
        pad_vectors()
        pl.semaphore_wait(barrier, k_count + w_count - 1 + ring)
        start(vec_relay(7, half, back))
        start(vec_relay(8, half_x, back))
        start(vec_full(0, fore, k))
        start(vec_full(1, back, k))
        start(vec_full(3, fore_x, k))
        start(vec_full(4, back_x, k))
        own_vecs.start()
        start(hr_copy)

    def second_window():
        start(vec_full(2, across, k))

    def third_window():
        start(vec_lower(5, half, k))
        start(vec_lower(6, half_x, k))
        vec_relay(7, half, back).wait_recv()
        start(vec_upper(9, back, fore))
        vec_relay(8, half_x, back).wait_recv()
        start(vec_upper(10, back_x, fore))

    def finish_first_window():
        own_vecs.wait()
        start(vec_forward(k))
        for slot, src in ((0, back), (1, fore), (3, back_x), (4, fore_x)):
            vec_full(slot, k, src).wait_recv()
            start(vec_forward(src))

    def finish_others():
        vec_full(2, k, across).wait_recv()
        start(vec_forward(across))
        for slots, src in (((5, 9), half), ((6, 10), half_x)):
            vec_lower(slots[0], k, src).wait_recv()
            vec_upper(slots[1], k, src).wait_recv()
            start(vec_forward(src))

    class Gather:
        def __init__(self, buf, sems, size):
            self.buf, self.sems = buf, sems
            self.halves = pl.ds(0, size // 2), pl.ds(size // 2, size - size // 2)

        def full(self, slot, src, dst):
            return remote(self.buf.at[src], self.buf.at[src], self.sems, slot, at_k(dst))

        def part(self, slot, src, dst):
            ref = self.buf.at[src, self.halves[slot % 2]]
            return remote(ref, ref, self.sems, slot, at_k(dst))

        def begin(self):
            start(self.full(8, k, across))
            start(self.full(0, k, fore))
            start(self.full(1, k, back))

        def middle(self, then=lambda: None):
            self.full(8, across, across).wait_recv()
            start(self.full(2, across, fore))
            start(self.full(3, across, back))
            then()
            self.full(0, back, fore).wait_recv()
            start(self.part(4, back, fore))
            self.full(1, fore, back).wait_recv()
            start(self.part(5, fore, back))
            self.full(2, back_x, fore).wait_recv()
            start(self.part(6, back_x, fore))
            self.full(3, fore_x, back).wait_recv()
            start(self.part(7, fore_x, back))

        def late(self):
            return ((half, (4, 5)), (half_x, (6, 7)))

        def wait_late(self, src, slots):
            for slot in slots:
                self.part(slot, src, fore).wait_recv()

    load_trial.wait()
    load_walkers.wait()
    green[...] = blocks_of_green(w_count, trial_ref, walkers_ref, first_window)

    def first_copy(d):
        dst = to_w(d)
        return remote(green.at[span(dst, SLOT)], first_buf.at[w], first_sems, d, at_near(dst))

    start_each(w_count, first_copy)
    first_buf[w] = green[span(w, SLOT), :]

    def aux_piece(which):
        shape = (per_w, aux_ref.shape[1])
        pick = jnp.where(iota(shape, 1) == walker_of(iota(shape, 0) + per_w * w, which), 1.0, 0.0)
        return dot(pick, aux_ref[...], ((1,), (1,)), HIGH)

    load_aux.wait()
    aux_out[...] = jnp.zeros_like(aux_out)
    aux_out[:, :vec_count] = aux_piece(other)
    start(aux_copy)
    aux_buf[core] = jnp.zeros(aux_buf.shape[1:], F32)
    aux_buf[core, :, :vec_count] = aux_piece(core)

    pick = permutation(
        each * per_k,
        w_count * SLOT,
        lambda r: lax.rem(r, per_k) // owned * SLOT + lax.rem(r, owned) * each + lax.div(r, per_k),
    )
    wide_f32[...] = jnp.zeros_like(wide_f32)
    each_of(w_count, lambda d: first_copy(d).wait_recv())
    picked = dot(pick, first_buf[...].reshape(w_count * SLOT, orbitals))
    for i in range(each):
        wide_f32[:, i * orbitals : (i + 1) * orbitals] = picked[i * per_k : (i + 1) * per_k, :]
    entries[k] = wide_f32[...].astype(BF16)
    gather = Gather(entries, entry_sems, per_k)
    gather.begin()
    hr_copy.wait_recv()
    gather.middle(second_window)
    for src, slots in gather.late():
        gather.wait_late(src, slots)
    partial[...] = dot(
        entries[...].reshape(rows, entries.shape[-1]), hr_buf[...].reshape(2 * gp, entries.shape[-1]), ((1,), (1,))
    )

    def partial_copy(d):
        dst = to_w(d)
        return remote(partial.at[span(block(dst, side), per_w)], partial_in.at[w], partial_sems, d, at_w(dst))

    start_each(w_count, partial_copy)
    third_window()
    partial_in[w] = partial[span(block(w, side), per_w), :]
    finish_first_window()
    aux_copy.wait_recv()
    aux = jnp.concatenate([aux_buf[0], aux_buf[1]], axis=1)
    each_of(w_count, lambda d: partial_copy(d).wait_recv())
    bias = jnp.sum(partial_in[...], axis=0)
    piece_b[...] = bias
    piece_f[...] = (aux - bias).astype(BF16)

    my_rows = span(w, per_w)

    def field_copy(d):
        dst = to_w(d)
        return remote(piece_f, fields.at[k, span(block(w, lax.div(dst, ring)), per_w)], field_w_sems, d, at_w(dst))

    start_each(w_count, field_copy)
    fields[k, span(block(w, side), per_w), :] = piece_f[...]

    def bias_copy(d):
        return remote(piece_b, bias_in.at[my_rows], bias_sems, d, at_w(to_w(d)))

    each_of(w_count, lambda d: field_copy(d).wait_recv())
    gather = Gather(fields, field_c_sems, rows)
    gather.begin()
    bias_in[my_rows, :] = piece_b[...]
    start_each(w_count, bias_copy)
    gather.middle()
    finish_others()

    def term(kk, columns):
        return dot(fields[kk], vecs_buf[kk, :, :, columns].reshape(2 * gp, part_width))

    def hop1(d, n):
        dst = to_k(d)
        return remote(out.at[n, span(dst, per_k)], one_in.at[n, k], hop1_sems, n * k_count + d, at_k(dst))

    def hop2(d, n):
        dst = to_w(d)
        return remote(two_out.at[n, span(dst, per_w)], result_ref.at[n, w], hop2_sems, n * w_count + d, at_near(dst))

    regroup = permutation(rows, rows, lambda r: lax.rem(lax.div(r, owned), k_count) * per_k + lax.div(r, per_w) * owned + lax.rem(r, owned))

    def own_result(n):
        return pltpu.make_async_copy(two_out.at[n, span(w, per_w)], result_ref.at[n, w], load_sems.at[5 + n])

    for step in range(CHUNKS + LAG):
        n = step
        if n < CHUNKS:
            columns = slice(n * part_width, (n + 1) * part_width)
            total = None
            for kk in (k, back, fore, back_x, fore_x, across, half, half_x):
                if n == 0:
                    vec_from_sibling(kk).wait_recv()
                    for src, slots in gather.late():
                        if kk is src:
                            gather.wait_late(src, slots)
                total = term(kk, columns) if total is None else total + term(kk, columns)
            out[n] = total.astype(BF16)
            start_each(k_count, functools.partial(hop1, n=n))
            one_in[n, k] = out[n, span(k, per_k), :]
        n = step - LAG
        if n >= 0:
            each_of(k_count, lambda d: hop1(d, n).wait_recv())
            two_out[n] = dot(regroup, one_in[n].reshape(rows, part_width)).astype(BF16)
            start_each(w_count, functools.partial(hop2, n=n))
            own_result(n).start()

    each_of(w_count, lambda d: bias_copy(d).wait_recv())
    low, high = bias_in[:, :gp], bias_in[:, gp:]
    bias_out[...] = jnp.where(core == 0, high, low)
    sib_copy = start(remote(bias_out, bias_sib, one_sems, 2, sibling))

    def spread(which):
        shape = (rows, bias_ref.shape[1])
        return jnp.where(iota(shape, 1) == walker_of(iota(shape, 0), which), 1.0, 0.0)

    mine = dot(jnp.where(core == 0, low, high), spread(core), ((0,), (0,)), HIGH)
    sib_copy.wait_recv()
    theirs = dot(bias_sib[...], spread(other), ((0,), (0,)), HIGH)
    bias_ref[...] = (mine + theirs)[:vec_count]
    bias_write = pltpu.make_async_copy(bias_ref, bias_hbm, load_sems.at[5 + CHUNKS])
    bias_write.start()

    for n in range(CHUNKS):
        each_of(w_count, lambda d: hop2(d, n).wait_recv())
        own_result(n).wait()
    bias_write.wait()
    for drain in drains:
        drain()


def taylor_kernel(k_count, walkers_hbm, pieces_hbm, bias_hbm, out_ref, bias_out, walkers_ref, pieces_ref, flat, stacked, sems):
    pairs = ((pieces_hbm, pieces_ref), (walkers_hbm, walkers_ref), (bias_hbm, bias_out))
    copies = [pltpu.make_async_copy(src, dst, sems.at[n]) for n, (src, dst) in enumerate(pairs)]
    for copy in copies:
        copy.start()
    owned, _, orbitals = walkers_ref.shape
    chunks, w_count, per_w, part_width = pieces_ref.shape
    width = chunks * part_width
    each = orbitals // w_count
    rows = w_count * per_w
    order = permutation(
        rows, rows, lambda r: lax.rem(r, w_count) * per_w + lax.rem(lax.div(r, w_count), k_count) * owned + lax.div(r, w_count * k_count)
    )
    for copy in copies[:2]:
        copy.wait()
    sorted_ = [dot(order, pieces_ref[n].reshape(rows, part_width)) for n in range(chunks)]
    place = permutation(orbitals, orbitals, lambda r: lax.rem(r, each) * w_count + lax.div(r, each))
    terms, totals, onebody = [], [], []
    for j in range(owned):
        for kk in range(k_count):
            at = (j * k_count + kk) * w_count
            for n in range(chunks):
                lane = kk * width + n * part_width
                flat[j, :, lane : lane + part_width] = sorted_[n][at : at + w_count, :]
        for q in range(each):
            stacked[j, q * w_count : (q + 1) * w_count, :] = flat[j, :, q * orbitals : (q + 1) * orbitals].astype(BF16)
        onebody.append(dot(stacked[j], place, ((0,), (1,))).astype(BF16))
        terms.append(walkers_ref[j])
        totals.append(walkers_ref[j])
    for step in range(1, TAYLOR + 1):
        for j in range(owned):
            head = terms[j].astype(BF16)
            rest = (terms[j] - head.astype(F32)).astype(BF16)
            terms[j] = (dot(head, onebody[j]) + dot(rest, onebody[j])) * (-1.0 / step)
            totals[j] = totals[j] + terms[j]
    for j in range(owned):
        out_ref[j] = totals[j]
    copies[2].wait()


def body(trial, walkers, aux_field, half_rotated, cholesky_vecs):
    k_count = lax.axis_size("chol") // 2
    w_count = lax.axis_size("walk")
    assert k_count == SIDE * LINE and w_count == SIDE * k_count
    owned, electrons, orbitals = walkers.shape
    vec_count, local_entries = half_rotated.shape
    walker_count = aux_field.shape[0]
    local_pairs = cholesky_vecs.shape[1]
    each = electrons // w_count
    gp = up(vec_count, 32)
    lanes = up(local_entries, 128)
    width = up(-(-local_pairs // k_count), 128 * CHUNKS)
    part_width = width // CHUNKS
    rows = k_count * w_count * owned
    per_k, per_w = w_count * owned, k_count * owned
    vmem = pl.BlockSpec(memory_space=pltpu.VMEM)
    hbm = pl.BlockSpec(memory_space=pltpu.HBM)
    dma = pltpu.SemaphoreType.DMA
    pieces, force_bias = pl.pallas_call(
        functools.partial(exchange_kernel, (k_count, w_count, owned, each, orbitals, vec_count)),
        out_shape=(
            jax.ShapeDtypeStruct((CHUNKS, w_count, per_w, part_width), BF16),
            jax.ShapeDtypeStruct((vec_count, walker_count), F32),
        ),
        in_specs=[hbm] * 5,
        out_specs=(hbm, hbm),
        scratch_shapes=[
            pltpu.VMEM(trial.shape, F32),
            pltpu.VMEM(walkers.shape, F32),
            pltpu.VMEM((vec_count, walker_count), F32),
            pltpu.VMEM(cholesky_vecs.shape, BF16),
            pltpu.VMEM(half_rotated.shape, BF16),
            pltpu.VMEM((vec_count, walker_count), F32),
            pltpu.VMEM((w_count * SLOT, orbitals), BF16),
            pltpu.VMEM((2, gp, lanes), BF16),
            pltpu.VMEM((per_w, gp), F32),
            pltpu.VMEM((2, per_w, gp), F32),
            pltpu.VMEM((gp, k_count * width), BF16),
            pltpu.VMEM((k_count, 2, gp, width), BF16),
            pltpu.VMEM((2, gp // 2, width), BF16),
            pltpu.VMEM((w_count, SLOT, orbitals), BF16),
            pltpu.VMEM((per_k, lanes), F32),
            pltpu.VMEM((k_count, per_k, lanes), BF16),
            pltpu.VMEM((rows, 2 * gp), F32),
            pltpu.VMEM((w_count, per_w, 2 * gp), F32),
            pltpu.VMEM((per_w, 2 * gp), BF16),
            pltpu.VMEM((per_w, 2 * gp), F32),
            pltpu.VMEM((k_count, rows, 2 * gp), BF16),
            pltpu.VMEM((rows, 2 * gp), F32),
            pltpu.VMEM((rows, gp), F32),
            pltpu.VMEM((rows, gp), F32),
            pltpu.VMEM((CHUNKS, rows, part_width), BF16),
            pltpu.VMEM((CHUNKS, k_count, per_k, part_width), BF16),
            pltpu.VMEM((CHUNKS, rows, part_width), BF16),
            dma((6 + CHUNKS,)),
            dma((3, 3)),
            dma((2, 11)),
            dma((2, k_count)),
            dma((2, w_count)),
            dma((2, 9)),
            dma((2, w_count)),
            dma((2, w_count)),
            dma((2, 9)),
            dma((2, w_count)),
            dma((2, CHUNKS * k_count)),
            dma((2, CHUNKS * w_count)),
        ],
        compiler_params=pltpu.CompilerParams(collective_id=0, has_side_effects=True, vmem_limit_bytes=VMEM_BYTES),
    )(trial, walkers, half_rotated, aux_field.T, cholesky_vecs)

    next_walkers, force_bias = pl.pallas_call(
        functools.partial(taylor_kernel, k_count),
        out_shape=(jax.ShapeDtypeStruct(walkers.shape, F32), jax.ShapeDtypeStruct(force_bias.shape, F32)),
        in_specs=[hbm, hbm, hbm],
        out_specs=(vmem, vmem),
        scratch_shapes=[
            pltpu.VMEM(walkers.shape, F32),
            pltpu.VMEM(pieces.shape, BF16),
            pltpu.VMEM((owned, w_count, k_count * width), F32),
            pltpu.VMEM((owned, orbitals, orbitals), BF16),
            dma((3,)),
        ],
        compiler_params=pltpu.CompilerParams(vmem_limit_bytes=VMEM_BYTES),
    )(walkers, pieces, force_bias)
    return (next_walkers, force_bias.T)


def solution(mesh):
    in_specs = (
        P(),
        P(("chol", "walk"), None, None),
        P(None, "chol"),
        P("chol", "walk"),
        P("chol", "walk"),
    )
    out_specs = (P(("chol", "walk"), None, None), P(None, "chol"))
    return jax.shard_map(body, mesh=mesh, in_specs=in_specs, out_specs=out_specs, check_vma=False)
```

```python
import functools

import jax
import jax.numpy as jnp
from jax import lax
from jax.experimental import pallas as pl
from jax.experimental.pallas import tpu as pltpu
from jax.sharding import PartitionSpec as P

TAYLOR = 6
SIDE, LINE = 2, 4
CHUNKS = 5
LAG = 2
HIGH = lax.Precision.HIGHEST
MESH = pl.DeviceIdType.MESH
F32 = jnp.float32
BF16 = jnp.bfloat16
VMEM_BYTES = 62 * 1024 * 1024
SLOT = 16


def up(value, multiple):
    return -(-value // multiple) * multiple


def iota(shape, dim):
    return lax.broadcasted_iota(jnp.int32, shape, dim)


def permutation(rows, cols, source):
    return jnp.where(iota((rows, cols), 1) == source(iota((rows, cols), 0)), 1.0, 0.0).astype(BF16)


def dot(a, b, contract=((1,), (0,)), precision=None):
    return lax.dot_general(a, b, (contract, ((), ())), preferred_element_type=F32, precision=precision)


def packed(value, block):
    rows = value.shape[0]
    tail = value[:, 256:].reshape(rows // block, 2, block // 2, 64)
    tail = jnp.concatenate([tail[:, 0], tail[:, 1]], axis=-1)
    parts = [value[:, :128].reshape(-1, block, 128), value[:, 128:256].reshape(-1, block, 128), tail]
    return jnp.concatenate(parts, axis=1)


def unpacked(value):
    block = value.shape[1] * 2 // 5
    tail = value[:, 2 * block :]
    tail = jnp.concatenate([tail[..., :64], tail[..., 64:]], axis=1)
    parts = [value[:, :block], value[:, block : 2 * block], tail]
    return jnp.concatenate(parts, axis=-1).reshape(-1, 320)


def invert(grams):
    size = grams[0].shape[0]
    rows = iota((size, size), 0)
    lanes = iota((1, size), 1)

    def pair(a, k):
        one = jnp.broadcast_to(a[:, k : k + 1], (size, size))
        two = jnp.broadcast_to(a[:, k + 1 : k + 2], (size, size))
        e11, e21, e12, e22 = one[k : k + 1], one[k + 1 : k + 2], two[k : k + 1], two[k + 1 : k + 2]
        first = 1.0 / e11
        right, below = first * e12, e21 * first
        p22 = 1.0 / (e22 - below * e12)
        p12, p21 = -right * p22, -p22 * below
        p11 = first + right * p22 * below
        upper = jnp.where(lanes == k, 1.0, jnp.where(lanes == k + 1, 0.0, a[k : k + 1]))
        lower = jnp.where(lanes == k, 0.0, jnp.where(lanes == k + 1, 1.0, a[k + 1 : k + 2]))
        upper, lower = p11 * upper + p12 * lower, p21 * upper + p22 * lower
        kept = jnp.where((lanes == k) | (lanes == k + 1), 0.0, a)
        return jnp.where(rows == k, upper, jnp.where(rows == k + 1, lower, kept - one * upper - two * lower))

    for k in range(0, size, 2):
        grams = [pair(a, k) for a in grams]
    return grams


def blocks_of_green(parts, trial_ref, walkers_ref, before_inverse):
    count, electrons, _ = walkers_ref.shape
    each = electrons // parts
    trial = trial_ref[...]
    walkers = [walkers_ref[j] for j in range(count)]
    corr = [dot(trial, w, ((1,), (1,)), HIGH) for w in walkers]
    grams = [dot(c, c, ((1,), (1,)), HIGH) for c in corr]
    before_inverse()
    rhs = [dot(c, w, precision=HIGH) for c, w in zip(corr, walkers)]
    inverse = invert(grams)
    green = [dot(g, r, precision=HIGH).astype(BF16) for g, r in zip(inverse, rhs)]
    total = None
    for j in range(count):

        def source(r):
            inside = r % SLOT - each * j
            return jnp.where((inside >= 0) & (inside < each), (r // SLOT) * each + inside, -1)

        part = dot(permutation(parts * SLOT, electrons, source), green[j])
        total = part if total is None else total + part
    return total.astype(BF16)


def exchange_kernel(
    dims,
    trial_hbm,
    walkers_hbm,
    hr_hbm,
    aux_hbm,
    vecs_hbm,
    result_ref,
    bias_hbm,
    trial_ref,
    walkers_ref,
    aux_ref,
    vecs_ref,
    hr_ref,
    bias_ref,
    green,
    hr_buf,
    aux_out,
    aux_buf,
    vecs_out,
    vecs_buf,
    relay,
    first_buf,
    wide_f32,
    entries,
    partial,
    partial_in,
    piece_f,
    piece_b,
    chip_fields,
    fields,
    bias_in,
    bias_out,
    bias_sib,
    out,
    one_in,
    two_out,
    load_sems,
    one_sems,
    vec_sems,
    fwd_sems,
    first_sems,
    entry_sems,
    partial_sems,
    field_w_sems,
    field_c_sems,
    bias_sems,
    hop1_sems,
    hop2_sems,
):
    k_count, w_count, owned, each, orbitals, vec_count = dims
    c = lax.axis_index("chol")
    w = lax.axis_index("walk")
    core = lax.rem(c, 2)
    k = lax.div(c, 2)
    other = 1 - core
    sibling = (2 * k + other, w)
    gp = hr_buf.shape[1]
    width = vecs_buf.shape[-1]
    part_width = width // CHUNKS
    rows = k_count * w_count * owned
    per_k = w_count * owned
    per_w = k_count * owned
    local_pairs = vecs_ref.shape[1]
    local_entries = hr_ref.shape[1]

    line = LINE * lax.div(k, LINE)
    across = lax.rem(k + LINE, k_count)
    line_across = lax.rem(line + LINE, k_count)

    def along(start, step):
        return start + lax.rem(k - line + step, LINE)

    fore, back, half = along(line, 1), along(line, LINE - 1), along(line, 2)
    fore_x, back_x, half_x = along(line_across, 1), along(line_across, LINE - 1), along(line_across, 2)

    def at_k(kk):
        return (2 * kk + core, w)

    def at_w(ww):
        return (c, ww)

    ring = w_count // SIDE
    side = lax.div(w, ring)

    def at_near(ww):
        return (2 * jnp.where(lax.div(ww, ring) == side, k, across) + core, ww)

    def block(piece, on_side):
        kk = lax.div(piece, SIDE)
        return SIDE * jnp.where(lax.rem(piece, SIDE) == on_side, kk, lax.rem(kk + LINE, k_count)) + lax.rem(piece, SIDE)

    def remote(src, dst, sems, slot, device):
        return pltpu.make_async_remote_copy(
            src_ref=src, dst_ref=dst, send_sem=sems.at[0, slot], recv_sem=sems.at[1, slot], device_id=device, device_id_type=MESH
        )

    drains = []

    def start(copy):
        copy.start()
        drains.append(copy.wait_send)
        return copy

    def each_of(count, body, first=1):
        def step(d, carry):
            body(d)
            return carry

        lax.fori_loop(first, count, step, 0)

    def start_each(count, make):
        each_of(count, lambda d: make(d).start())
        drains.append(lambda: each_of(count, lambda d: make(d).wait_send()))

    def to_k(d):
        return lax.rem(k + d, k_count)

    def to_w(d):
        return lax.rem(w + d, w_count)

    def walker_of(row, which):
        return per_k * (2 * lax.div(row, per_k) + which) + lax.rem(row, per_k)

    def span(index, size):
        return pl.ds(pl.multiple_of(index * size, size), size)

    pairs = ((trial_hbm, trial_ref), (walkers_hbm, walkers_ref), (aux_hbm, aux_ref), (vecs_hbm, vecs_ref), (hr_hbm, hr_ref))
    load_trial, load_walkers, load_aux, load_vecs, load_hr = loads = [
        pltpu.make_async_copy(src, dst, load_sems.at[n]) for n, (src, dst) in enumerate(pairs)
    ]
    for load in loads:
        load.start()

    barrier = pltpu.get_barrier_semaphore()
    each_of(k_count, lambda d: pl.semaphore_signal(barrier, inc=1, device_id=at_k(to_k(d)), device_id_type=MESH))
    each_of(w_count, lambda d: pl.semaphore_signal(barrier, inc=1, device_id=at_w(to_w(d)), device_id_type=MESH))
    opposite = ring * (SIDE - 1 - side)
    each_of(ring, lambda d: pl.semaphore_signal(barrier, inc=1, device_id=at_near(opposite + d), device_id_type=MESH), 0)
    pl.semaphore_signal(barrier, inc=1, device_id=sibling, device_id_type=MESH)

    def pad_vectors():
        edge = local_pairs // 128 * 128
        vecs_out[gp - 16 :, :] = jnp.zeros((16, vecs_out.shape[1]), BF16)
        if edge < vecs_out.shape[1]:
            vecs_out[:, edge:] = jnp.zeros((gp, vecs_out.shape[1] - edge), BF16)
        load_vecs.wait()
        vecs_out[:vec_count, :local_pairs] = vecs_ref[...]
        hr_buf[core] = jnp.zeros(hr_buf.shape[1:], BF16)
        load_hr.wait()
        hr_buf[core, :vec_count, :local_entries] = hr_ref[...]

    cut = gp // 2
    lower, upper = pl.ds(0, cut), pl.ds(cut, gp - cut)

    def vec_full(slot, dst, src):
        return remote(vecs_out.at[:, span(dst, width)], vecs_buf.at[src, core], vec_sems, slot, at_k(dst))

    def vec_lower(slot, dst, src):
        return remote(vecs_out.at[lower, span(dst, width)], vecs_buf.at[src, core, lower], vec_sems, slot, at_k(dst))

    def vec_relay(slot, dst, by):
        return remote(vecs_out.at[upper, span(dst, width)], relay.at[slot - 7], vec_sems, slot, at_k(by))

    def vec_upper(slot, dst, src):
        return remote(relay.at[slot - 9], vecs_buf.at[src, core, upper], vec_sems, slot, at_k(dst))

    def vec_forward(kk):
        return remote(vecs_buf.at[kk, core], vecs_buf.at[kk, core], fwd_sems, kk, sibling)

    def vec_from_sibling(kk):
        return remote(vecs_buf.at[kk, other], vecs_buf.at[kk, other], fwd_sems, kk, sibling)

    own_vecs = pltpu.make_async_copy(vecs_out.at[:, span(k, width)], vecs_buf.at[k, core], one_sems.at[2, 0])
    hr_copy = remote(hr_buf.at[core], hr_buf.at[core], one_sems, 0, sibling)
    aux_copy = remote(aux_out, aux_buf.at[core], one_sems, 1, sibling)

    def first_window():
        pad_vectors()
        pl.semaphore_wait(barrier, k_count + w_count - 1 + ring)
        start(vec_relay(7, half, back))
        start(vec_relay(8, half_x, back))
        start(vec_full(0, fore, k))
        start(vec_full(1, back, k))
        start(vec_full(3, fore_x, k))
        start(vec_full(4, back_x, k))
        own_vecs.start()
        start(hr_copy)

    def second_window():
        start(vec_full(2, across, k))

    def third_window():
        start(vec_lower(5, half, k))
        start(vec_lower(6, half_x, k))
        vec_relay(7, half, back).wait_recv()
        start(vec_upper(9, back, fore))
        vec_relay(8, half_x, back).wait_recv()
        start(vec_upper(10, back_x, fore))

    def finish_first_window():
        own_vecs.wait()
        start(vec_forward(k))
        for slot, src in ((0, back), (1, fore), (3, back_x), (4, fore_x)):
            vec_full(slot, k, src).wait_recv()
            start(vec_forward(src))

    def finish_others():
        vec_full(2, k, across).wait_recv()
        start(vec_forward(across))
        for slots, src in (((5, 9), half), ((6, 10), half_x)):
            vec_lower(slots[0], k, src).wait_recv()
            vec_upper(slots[1], k, src).wait_recv()
            start(vec_forward(src))

    class Gather:
        def __init__(self, buf, sems, size):
            self.buf, self.sems = buf, sems
            self.halves = pl.ds(0, size // 2), pl.ds(size // 2, size - size // 2)

        def full(self, slot, src, dst):
            return remote(self.buf.at[src], self.buf.at[src], self.sems, slot, at_k(dst))

        def part(self, slot, src, dst):
            ref = self.buf.at[src, self.halves[slot % 2]]
            return remote(ref, ref, self.sems, slot, at_k(dst))

        def begin(self):
            start(self.full(8, k, across))
            start(self.full(0, k, fore))
            start(self.full(1, k, back))

        def middle(self, then=lambda: None):
            self.full(8, across, across).wait_recv()
            start(self.full(2, across, fore))
            start(self.full(3, across, back))
            then()
            self.full(0, back, fore).wait_recv()
            start(self.part(4, back, fore))
            self.full(1, fore, back).wait_recv()
            start(self.part(5, fore, back))
            self.full(2, back_x, fore).wait_recv()
            start(self.part(6, back_x, fore))
            self.full(3, fore_x, back).wait_recv()
            start(self.part(7, fore_x, back))

        def late(self):
            return ((half, (4, 5)), (half_x, (6, 7)))

        def wait_late(self, src, slots):
            for slot in slots:
                self.part(slot, src, fore).wait_recv()

    load_trial.wait()
    load_walkers.wait()
    green[...] = blocks_of_green(w_count, trial_ref, walkers_ref, first_window)

    def first_copy(d):
        dst = to_w(d)
        return remote(green.at[span(dst, SLOT)], first_buf.at[w], first_sems, d, at_near(dst))

    start_each(w_count, first_copy)
    first_buf[w] = green[span(w, SLOT), :]

    def aux_piece(which):
        shape = (per_w, aux_ref.shape[1])
        pick = jnp.where(iota(shape, 1) == walker_of(iota(shape, 0) + per_w * w, which), 1.0, 0.0)
        return dot(pick, aux_ref[...], ((1,), (1,)), HIGH)

    load_aux.wait()
    aux_out[...] = jnp.zeros_like(aux_out)
    aux_out[:, :vec_count] = aux_piece(other)
    start(aux_copy)
    aux_buf[core] = jnp.zeros(aux_buf.shape[1:], F32)
    aux_buf[core, :, :vec_count] = aux_piece(core)

    pick = permutation(
        each * per_k,
        w_count * SLOT,
        lambda r: lax.rem(r, per_k) // owned * SLOT + lax.rem(r, owned) * each + lax.div(r, per_k),
    )
    wide_f32[...] = jnp.zeros_like(wide_f32)
    each_of(w_count, lambda d: first_copy(d).wait_recv())
    picked = dot(pick, first_buf[...].reshape(w_count * SLOT, orbitals))
    for i in range(each):
        wide_f32[:, i * orbitals : (i + 1) * orbitals] = picked[i * per_k : (i + 1) * per_k, :]
    entries[k] = wide_f32[...].astype(BF16)
    gather = Gather(entries, entry_sems, per_k)
    gather.begin()
    hr_copy.wait_recv()
    gather.middle(second_window)
    for src, slots in gather.late():
        gather.wait_late(src, slots)
    sums = dot(entries[...].reshape(rows, entries.shape[-1]), hr_buf[...].reshape(2 * gp, entries.shape[-1]), ((1,), (1,)))
    partial[...] = packed(sums, per_w)

    def partial_copy(d):
        dst = to_w(d)
        return remote(partial.at[block(dst, side)], partial_in.at[w], partial_sems, d, at_w(dst))

    start_each(w_count, partial_copy)
    third_window()
    partial_in[w] = partial[block(w, side)]
    finish_first_window()
    aux_copy.wait_recv()
    aux = jnp.concatenate([aux_buf[0], aux_buf[1]], axis=1)
    each_of(w_count, lambda d: partial_copy(d).wait_recv())
    bias = jnp.sum(partial_in[...], axis=0)
    piece_b[...] = bias
    piece_f[...] = (aux - unpacked(bias[None])).astype(BF16)

    def field_copy(d):
        dst = to_w(d)
        return remote(piece_f, chip_fields.at[span(block(w, lax.div(dst, ring)), per_w)], field_w_sems, d, at_w(dst))

    start_each(w_count, field_copy)
    chip_fields[span(block(w, side), per_w), :] = piece_f[...]

    def bias_copy(d):
        return remote(piece_b, bias_in.at[w], bias_sems, d, at_w(to_w(d)))

    each_of(w_count, lambda d: field_copy(d).wait_recv())
    fields[k] = packed(chip_fields[...], rows)[0]
    gather = Gather(fields, field_c_sems, fields.shape[1])
    gather.begin()
    bias_in[w] = piece_b[...]
    gather.middle(lambda: start_each(w_count, bias_copy))
    finish_others()

    def term(kk, columns):
        return dot(unpacked(fields[kk][None]), vecs_buf[kk, :, :, columns].reshape(2 * gp, part_width))

    def hop1(d, n):
        dst = to_k(d)
        return remote(out.at[n, span(dst, per_k)], one_in.at[n, k], hop1_sems, n * k_count + d, at_k(dst))

    def hop2(d, n):
        dst = to_w(d)
        return remote(two_out.at[n, span(dst, per_w)], result_ref.at[n, w], hop2_sems, n * w_count + d, at_near(dst))

    regroup = permutation(rows, rows, lambda r: lax.rem(lax.div(r, owned), k_count) * per_k + lax.div(r, per_w) * owned + lax.rem(r, owned))

    def own_result(n):
        return pltpu.make_async_copy(two_out.at[n, span(w, per_w)], result_ref.at[n, w], load_sems.at[5 + n])

    for step in range(CHUNKS + LAG):
        n = step
        if n < CHUNKS:
            columns = slice(n * part_width, (n + 1) * part_width)
            total = None
            for kk in (k, back, fore, back_x, fore_x, across, half, half_x):
                if n == 0:
                    vec_from_sibling(kk).wait_recv()
                    for src, slots in gather.late():
                        if kk is src:
                            gather.wait_late(src, slots)
                total = term(kk, columns) if total is None else total + term(kk, columns)
            out[n] = total.astype(BF16)
            start_each(k_count, functools.partial(hop1, n=n))
            one_in[n, k] = out[n, span(k, per_k), :]
        n = step - LAG
        if n >= 0:
            each_of(k_count, lambda d: hop1(d, n).wait_recv())
            two_out[n] = dot(regroup, one_in[n].reshape(rows, part_width)).astype(BF16)
            start_each(w_count, functools.partial(hop2, n=n))
            own_result(n).start()

    each_of(w_count, lambda d: bias_copy(d).wait_recv())
    sums = unpacked(bias_in[...])
    low, high = sums[:, :gp], sums[:, gp:]
    bias_out[...] = jnp.where(core == 0, high, low)
    sib_copy = start(remote(bias_out, bias_sib, one_sems, 2, sibling))

    def spread(which):
        shape = (rows, bias_ref.shape[1])
        return jnp.where(iota(shape, 1) == walker_of(iota(shape, 0), which), 1.0, 0.0)

    mine = dot(jnp.where(core == 0, low, high), spread(core), ((0,), (0,)), HIGH)
    sib_copy.wait_recv()
    theirs = dot(bias_sib[...], spread(other), ((0,), (0,)), HIGH)
    bias_ref[...] = (mine + theirs)[:vec_count]
    bias_write = pltpu.make_async_copy(bias_ref, bias_hbm, load_sems.at[5 + CHUNKS])
    bias_write.start()

    for n in range(CHUNKS):
        each_of(w_count, lambda d: hop2(d, n).wait_recv())
        own_result(n).wait()
    bias_write.wait()
    for drain in drains:
        drain()


def taylor_kernel(k_count, walkers_hbm, pieces_hbm, bias_hbm, out_ref, bias_out, walkers_ref, pieces_ref, flat, stacked, sems):
    pairs = ((pieces_hbm, pieces_ref), (walkers_hbm, walkers_ref), (bias_hbm, bias_out))
    copies = [pltpu.make_async_copy(src, dst, sems.at[n]) for n, (src, dst) in enumerate(pairs)]
    for copy in copies:
        copy.start()
    owned, _, orbitals = walkers_ref.shape
    chunks, w_count, per_w, part_width = pieces_ref.shape
    width = chunks * part_width
    each = orbitals // w_count
    rows = w_count * per_w
    order = permutation(
        rows, rows, lambda r: lax.rem(r, w_count) * per_w + lax.rem(lax.div(r, w_count), k_count) * owned + lax.div(r, w_count * k_count)
    )
    for copy in copies[:2]:
        copy.wait()
    sorted_ = [dot(order, pieces_ref[n].reshape(rows, part_width)) for n in range(chunks)]
    place = permutation(orbitals, orbitals, lambda r: lax.rem(r, each) * w_count + lax.div(r, each))
    terms, totals, onebody = [], [], []
    for j in range(owned):
        for kk in range(k_count):
            at = (j * k_count + kk) * w_count
            for n in range(chunks):
                lane = kk * width + n * part_width
                flat[j, :, lane : lane + part_width] = sorted_[n][at : at + w_count, :]
        for q in range(each):
            stacked[j, q * w_count : (q + 1) * w_count, :] = flat[j, :, q * orbitals : (q + 1) * orbitals].astype(BF16)
        onebody.append(dot(stacked[j], place, ((0,), (1,))).astype(BF16))
        terms.append(walkers_ref[j])
        totals.append(walkers_ref[j])
    for step in range(1, TAYLOR + 1):
        for j in range(owned):
            head = terms[j].astype(BF16)
            rest = (terms[j] - head.astype(F32)).astype(BF16)
            terms[j] = (dot(head, onebody[j]) + dot(rest, onebody[j])) * (-1.0 / step)
            totals[j] = totals[j] + terms[j]
    for j in range(owned):
        out_ref[j] = totals[j]
    copies[2].wait()


def body(trial, walkers, aux_field, half_rotated, cholesky_vecs):
    k_count = lax.axis_size("chol") // 2
    w_count = lax.axis_size("walk")
    assert k_count == SIDE * LINE and w_count == SIDE * k_count and 256 < 2 * up(half_rotated.shape[0], 32) == 320
    owned, electrons, orbitals = walkers.shape
    vec_count, local_entries = half_rotated.shape
    walker_count = aux_field.shape[0]
    local_pairs = cholesky_vecs.shape[1]
    each = electrons // w_count
    gp = up(vec_count, 32)
    lanes = up(local_entries, 128)
    width = up(-(-local_pairs // k_count), 128 * CHUNKS)
    part_width = width // CHUNKS
    rows = k_count * w_count * owned
    per_k, per_w = w_count * owned, k_count * owned
    vmem = pl.BlockSpec(memory_space=pltpu.VMEM)
    hbm = pl.BlockSpec(memory_space=pltpu.HBM)
    dma = pltpu.SemaphoreType.DMA
    pieces, force_bias = pl.pallas_call(
        functools.partial(exchange_kernel, (k_count, w_count, owned, each, orbitals, vec_count)),
        out_shape=(
            jax.ShapeDtypeStruct((CHUNKS, w_count, per_w, part_width), BF16),
            jax.ShapeDtypeStruct((vec_count, walker_count), F32),
        ),
        in_specs=[hbm] * 5,
        out_specs=(hbm, hbm),
        scratch_shapes=[
            pltpu.VMEM(trial.shape, F32),
            pltpu.VMEM(walkers.shape, F32),
            pltpu.VMEM((vec_count, walker_count), F32),
            pltpu.VMEM(cholesky_vecs.shape, BF16),
            pltpu.VMEM(half_rotated.shape, BF16),
            pltpu.VMEM((vec_count, walker_count), F32),
            pltpu.VMEM((w_count * SLOT, orbitals), BF16),
            pltpu.VMEM((2, gp, lanes), BF16),
            pltpu.VMEM((per_w, gp), F32),
            pltpu.VMEM((2, per_w, gp), F32),
            pltpu.VMEM((gp, k_count * width), BF16),
            pltpu.VMEM((k_count, 2, gp, width), BF16),
            pltpu.VMEM((2, gp // 2, width), BF16),
            pltpu.VMEM((w_count, SLOT, orbitals), BF16),
            pltpu.VMEM((per_k, lanes), F32),
            pltpu.VMEM((k_count, per_k, lanes), BF16),
            pltpu.VMEM((w_count, per_w * 5 // 2, 128), F32),
            pltpu.VMEM((w_count, per_w * 5 // 2, 128), F32),
            pltpu.VMEM((per_w, 2 * gp), BF16),
            pltpu.VMEM((per_w * 5 // 2, 128), F32),
            pltpu.VMEM((rows, 2 * gp), BF16),
            pltpu.VMEM((k_count, rows * 5 // 2, 128), BF16),
            pltpu.VMEM((w_count, per_w * 5 // 2, 128), F32),
            pltpu.VMEM((rows, gp), F32),
            pltpu.VMEM((rows, gp), F32),
            pltpu.VMEM((CHUNKS, rows, part_width), BF16),
            pltpu.VMEM((CHUNKS, k_count, per_k, part_width), BF16),
            pltpu.VMEM((CHUNKS, rows, part_width), BF16),
            dma((6 + CHUNKS,)),
            dma((3, 3)),
            dma((2, 11)),
            dma((2, k_count)),
            dma((2, w_count)),
            dma((2, 9)),
            dma((2, w_count)),
            dma((2, w_count)),
            dma((2, 9)),
            dma((2, w_count)),
            dma((2, CHUNKS * k_count)),
            dma((2, CHUNKS * w_count)),
        ],
        compiler_params=pltpu.CompilerParams(collective_id=0, has_side_effects=True, vmem_limit_bytes=VMEM_BYTES),
    )(trial, walkers, half_rotated, aux_field.T, cholesky_vecs)

    next_walkers, force_bias = pl.pallas_call(
        functools.partial(taylor_kernel, k_count),
        out_shape=(jax.ShapeDtypeStruct(walkers.shape, F32), jax.ShapeDtypeStruct(force_bias.shape, F32)),
        in_specs=[hbm, hbm, hbm],
        out_specs=(vmem, vmem),
        scratch_shapes=[
            pltpu.VMEM(walkers.shape, F32),
            pltpu.VMEM(pieces.shape, BF16),
            pltpu.VMEM((owned, w_count, k_count * width), F32),
            pltpu.VMEM((owned, orbitals, orbitals), BF16),
            dma((3,)),
        ],
        compiler_params=pltpu.CompilerParams(vmem_limit_bytes=VMEM_BYTES),
    )(walkers, pieces, force_bias)
    return (next_walkers, force_bias.T)


def solution(mesh):
    in_specs = (
        P(),
        P(("chol", "walk"), None, None),
        P(None, "chol"),
        P("chol", "walk"),
        P("chol", "walk"),
    )
    out_specs = (P(("chol", "walk"), None, None), P(None, "chol"))
    return jax.shard_map(body, mesh=mesh, in_specs=in_specs, out_specs=out_specs, check_vma=False)
```

```python
import functools

import jax
import jax.numpy as jnp
from jax import lax
from jax.experimental import pallas as pl
from jax.experimental.pallas import tpu as pltpu
from jax.sharding import PartitionSpec as P

TAYLOR = 6
SIDE, LINE = 2, 4
CHUNKS = 5
LAG = 3
HIGH = lax.Precision.HIGHEST
MESH = pl.DeviceIdType.MESH
F32 = jnp.float32
BF16 = jnp.bfloat16
VMEM_BYTES = 62 * 1024 * 1024
SLOT = 16


def up(value, multiple):
    return -(-value // multiple) * multiple


def iota(shape, dim):
    return lax.broadcasted_iota(jnp.int32, shape, dim)


def permutation(rows, cols, source):
    return jnp.where(iota((rows, cols), 1) == source(iota((rows, cols), 0)), 1.0, 0.0).astype(BF16)


def dot(a, b, contract=((1,), (0,)), precision=None):
    return lax.dot_general(a, b, (contract, ((), ())), preferred_element_type=F32, precision=precision)


def packed(value, block):
    rows = value.shape[0]
    tail = value[:, 256:].reshape(rows // block, 2, block // 2, 64)
    tail = jnp.concatenate([tail[:, 0], tail[:, 1]], axis=-1)
    parts = [value[:, :128].reshape(-1, block, 128), value[:, 128:256].reshape(-1, block, 128), tail]
    return jnp.concatenate(parts, axis=1)


def unpacked(value):
    block = value.shape[1] * 2 // 5
    tail = value[:, 2 * block :]
    tail = jnp.concatenate([tail[..., :64], tail[..., 64:]], axis=1)
    parts = [value[:, :block], value[:, block : 2 * block], tail]
    return jnp.concatenate(parts, axis=-1).reshape(-1, 320)


def invert(grams):
    size = grams[0].shape[0]
    rows = iota((size, size), 0)
    lanes = iota((1, size), 1)

    def pair(a, k):
        one = jnp.broadcast_to(a[:, k : k + 1], (size, size))
        two = jnp.broadcast_to(a[:, k + 1 : k + 2], (size, size))
        e11, e21, e12, e22 = one[k : k + 1], one[k + 1 : k + 2], two[k : k + 1], two[k + 1 : k + 2]
        first = 1.0 / e11
        right, below = first * e12, e21 * first
        p22 = 1.0 / (e22 - below * e12)
        p12, p21 = -right * p22, -p22 * below
        p11 = first + right * p22 * below
        upper = jnp.where(lanes == k, 1.0, jnp.where(lanes == k + 1, 0.0, a[k : k + 1]))
        lower = jnp.where(lanes == k, 0.0, jnp.where(lanes == k + 1, 1.0, a[k + 1 : k + 2]))
        upper, lower = p11 * upper + p12 * lower, p21 * upper + p22 * lower
        kept = jnp.where((lanes == k) | (lanes == k + 1), 0.0, a)
        return jnp.where(rows == k, upper, jnp.where(rows == k + 1, lower, kept - one * upper - two * lower))

    for k in range(0, size, 2):
        grams = [pair(a, k) for a in grams]
    return grams


def blocks_of_green(parts, trial_ref, walkers_ref, before_inverse):
    count, electrons, _ = walkers_ref.shape
    each = electrons // parts
    trial = trial_ref[...]
    walkers = [walkers_ref[j] for j in range(count)]
    corr = [dot(trial, w, ((1,), (1,)), HIGH) for w in walkers]
    grams = [dot(c, c, ((1,), (1,)), HIGH) for c in corr]
    rhs = [dot(c, w, precision=HIGH) for c, w in zip(corr, walkers)]
    before_inverse()
    inverse = invert(grams)
    green = [dot(g, r, precision=HIGH).astype(BF16) for g, r in zip(inverse, rhs)]
    total = None
    for j in range(count):

        def source(r):
            inside = r % SLOT - each * j
            return jnp.where((inside >= 0) & (inside < each), (r // SLOT) * each + inside, -1)

        part = dot(permutation(parts * SLOT, electrons, source), green[j])
        total = part if total is None else total + part
    return total.astype(BF16)


def exchange_kernel(
    dims,
    trial_hbm,
    walkers_hbm,
    hr_hbm,
    aux_hbm,
    vecs_hbm,
    result_ref,
    bias_hbm,
    trial_ref,
    walkers_ref,
    aux_ref,
    vecs_ref,
    hr_ref,
    bias_ref,
    green,
    hr_buf,
    aux_out,
    aux_buf,
    vecs_out,
    vecs_buf,
    relay,
    first_buf,
    wide_f32,
    entries,
    partial,
    partial_in,
    piece_f,
    piece_b,
    chip_fields,
    fields,
    whole_fields,
    bias_in,
    bias_out,
    bias_sib,
    out,
    one_in,
    two_out,
    load_sems,
    one_sems,
    vec_sems,
    fwd_sems,
    first_sems,
    entry_sems,
    partial_sems,
    field_w_sems,
    field_c_sems,
    bias_sems,
    hop1_sems,
    hop2_sems,
):
    k_count, w_count, owned, each, orbitals, vec_count = dims
    c = lax.axis_index("chol")
    w = lax.axis_index("walk")
    core = lax.rem(c, 2)
    k = lax.div(c, 2)
    other = 1 - core
    sibling = (2 * k + other, w)
    gp = hr_buf.shape[1]
    width = vecs_buf.shape[-1]
    part_width = width // CHUNKS
    rows = k_count * w_count * owned
    per_k = w_count * owned
    per_w = k_count * owned
    local_pairs = vecs_ref.shape[1]
    local_entries = hr_ref.shape[1]

    line = LINE * lax.div(k, LINE)
    across = lax.rem(k + LINE, k_count)
    line_across = lax.rem(line + LINE, k_count)

    def along(start, step):
        return start + lax.rem(k - line + step, LINE)

    fore, back, half = along(line, 1), along(line, LINE - 1), along(line, 2)
    fore_x, back_x, half_x = along(line_across, 1), along(line_across, LINE - 1), along(line_across, 2)

    def at_k(kk):
        return (2 * kk + core, w)

    def at_w(ww):
        return (c, ww)

    ring = w_count // SIDE
    side = lax.div(w, ring)

    def at_near(ww):
        return (2 * jnp.where(lax.div(ww, ring) == side, k, across) + core, ww)

    def block(piece, on_side):
        kk = lax.div(piece, SIDE)
        return SIDE * jnp.where(lax.rem(piece, SIDE) == on_side, kk, lax.rem(kk + LINE, k_count)) + lax.rem(piece, SIDE)

    def remote(src, dst, sems, slot, device):
        return pltpu.make_async_remote_copy(
            src_ref=src, dst_ref=dst, send_sem=sems.at[0, slot], recv_sem=sems.at[1, slot], device_id=device, device_id_type=MESH
        )

    drains = []

    def start(copy):
        copy.start()
        drains.append(copy.wait_send)
        return copy

    def each_of(count, body, first=1):
        def step(d, carry):
            body(d)
            return carry

        lax.fori_loop(first, count, step, 0)

    def start_each(count, make):
        each_of(count, lambda d: make(d).start())
        drains.append(lambda: each_of(count, lambda d: make(d).wait_send()))

    def to_k(d):
        return lax.rem(k + d, k_count)

    def to_w(d):
        return lax.rem(w + d, w_count)

    def walker_of(row, which):
        return per_k * (2 * lax.div(row, per_k) + which) + lax.rem(row, per_k)

    def span(index, size):
        return pl.ds(pl.multiple_of(index * size, size), size)

    pairs = ((trial_hbm, trial_ref), (walkers_hbm, walkers_ref), (aux_hbm, aux_ref), (vecs_hbm, vecs_ref), (hr_hbm, hr_ref))
    load_trial, load_walkers, load_aux, load_vecs, load_hr = loads = [
        pltpu.make_async_copy(src, dst, load_sems.at[n]) for n, (src, dst) in enumerate(pairs)
    ]
    for load in loads:
        load.start()

    barrier = pltpu.get_barrier_semaphore()
    each_of(k_count, lambda d: pl.semaphore_signal(barrier, inc=1, device_id=at_k(to_k(d)), device_id_type=MESH))
    each_of(w_count, lambda d: pl.semaphore_signal(barrier, inc=1, device_id=at_w(to_w(d)), device_id_type=MESH))
    opposite = ring * (SIDE - 1 - side)
    each_of(ring, lambda d: pl.semaphore_signal(barrier, inc=1, device_id=at_near(opposite + d), device_id_type=MESH), 0)
    pl.semaphore_signal(barrier, inc=1, device_id=sibling, device_id_type=MESH)

    def pad_vectors():
        edge = local_pairs // 128 * 128
        vecs_out[gp - 16 :, :] = jnp.zeros((16, vecs_out.shape[1]), BF16)
        if edge < vecs_out.shape[1]:
            vecs_out[:, edge:] = jnp.zeros((gp, vecs_out.shape[1] - edge), BF16)
        load_vecs.wait()
        vecs_out[:vec_count, :local_pairs] = vecs_ref[...]
        hr_buf[core] = jnp.zeros(hr_buf.shape[1:], BF16)
        load_hr.wait()
        hr_buf[core, :vec_count, :local_entries] = hr_ref[...]

    cut = gp // 2
    lower, upper = pl.ds(0, cut), pl.ds(cut, gp - cut)

    def vec_full(slot, dst, src):
        return remote(vecs_out.at[:, span(dst, width)], vecs_buf.at[src, core], vec_sems, slot, at_k(dst))

    def vec_lower(slot, dst, src):
        return remote(vecs_out.at[lower, span(dst, width)], vecs_buf.at[src, core, lower], vec_sems, slot, at_k(dst))

    def vec_relay(slot, dst, by):
        return remote(vecs_out.at[upper, span(dst, width)], relay.at[slot - 7], vec_sems, slot, at_k(by))

    def vec_upper(slot, dst, src):
        return remote(relay.at[slot - 9], vecs_buf.at[src, core, upper], vec_sems, slot, at_k(dst))

    def vec_forward(kk):
        return remote(vecs_buf.at[kk, core], vecs_buf.at[kk, core], fwd_sems, kk, sibling)

    def vec_from_sibling(kk):
        return remote(vecs_buf.at[kk, other], vecs_buf.at[kk, other], fwd_sems, kk, sibling)

    own_vecs = pltpu.make_async_copy(vecs_out.at[:, span(k, width)], vecs_buf.at[k, core], one_sems.at[2, 0])
    hr_copy = remote(hr_buf.at[core], hr_buf.at[core], one_sems, 0, sibling)
    aux_copy = remote(aux_out, aux_buf.at[core], one_sems, 1, sibling)

    def first_window():
        pad_vectors()
        pl.semaphore_wait(barrier, k_count + w_count - 1 + ring)
        start(vec_relay(7, half, back))
        start(vec_relay(8, half_x, back))
        start(vec_full(0, fore, k))
        start(vec_full(1, back, k))
        start(vec_full(3, fore_x, k))
        start(vec_full(4, back_x, k))
        own_vecs.start()
        start(hr_copy)

    def second_window():
        start(vec_full(2, across, k))

    def third_window():
        start(vec_lower(5, half, k))
        start(vec_lower(6, half_x, k))
        vec_relay(7, half, back).wait_recv()
        start(vec_upper(9, back, fore))
        vec_relay(8, half_x, back).wait_recv()
        start(vec_upper(10, back_x, fore))

    def finish_first_window():
        own_vecs.wait()
        start(vec_forward(k))
        for slot, src in ((0, back), (1, fore), (3, back_x), (4, fore_x)):
            vec_full(slot, k, src).wait_recv()
            start(vec_forward(src))

    def finish_others():
        vec_full(2, k, across).wait_recv()
        start(vec_forward(across))
        for slots, src in (((5, 9), half), ((6, 10), half_x)):
            vec_lower(slots[0], k, src).wait_recv()
            vec_upper(slots[1], k, src).wait_recv()
            start(vec_forward(src))

    class Gather:
        def __init__(self, buf, sems, size):
            self.buf, self.sems = buf, sems
            self.halves = pl.ds(0, size // 2), pl.ds(size // 2, size - size // 2)

        def full(self, slot, src, dst):
            return remote(self.buf.at[src], self.buf.at[src], self.sems, slot, at_k(dst))

        def part(self, slot, src, dst):
            ref = self.buf.at[src, self.halves[slot % 2]]
            return remote(ref, ref, self.sems, slot, at_k(dst))

        def begin(self):
            start(self.full(8, k, across))
            start(self.full(0, k, fore))
            start(self.full(1, k, back))

        def middle(self, then=lambda: None):
            self.full(8, across, across).wait_recv()
            start(self.full(2, across, fore))
            start(self.full(3, across, back))
            then()
            self.full(0, back, fore).wait_recv()
            start(self.part(4, back, fore))
            self.full(1, fore, back).wait_recv()
            start(self.part(5, fore, back))
            self.full(2, back_x, fore).wait_recv()
            start(self.part(6, back_x, fore))
            self.full(3, fore_x, back).wait_recv()
            start(self.part(7, fore_x, back))

        def late(self):
            return ((half, (4, 5)), (half_x, (6, 7)))

        def wait_late(self, src, slots):
            for slot in slots:
                self.part(slot, src, fore).wait_recv()

    load_trial.wait()
    load_walkers.wait()
    green[...] = blocks_of_green(w_count, trial_ref, walkers_ref, first_window)

    def first_copy(d):
        dst = to_w(d)
        return remote(green.at[span(dst, SLOT)], first_buf.at[w], first_sems, d, at_near(dst))

    start_each(w_count, first_copy)
    first_buf[w] = green[span(w, SLOT), :]

    def aux_piece(which):
        shape = (per_w, aux_ref.shape[1])
        pick = jnp.where(iota(shape, 1) == walker_of(iota(shape, 0) + per_w * w, which), 1.0, 0.0)
        return dot(pick, aux_ref[...], ((1,), (1,)), HIGH)

    load_aux.wait()
    aux_out[...] = jnp.zeros_like(aux_out)
    aux_out[:, :vec_count] = aux_piece(other)
    start(aux_copy)
    aux_buf[core] = jnp.zeros(aux_buf.shape[1:], F32)
    aux_buf[core, :, :vec_count] = aux_piece(core)

    pick = permutation(
        each * per_k,
        w_count * SLOT,
        lambda r: lax.rem(r, per_k) // owned * SLOT + lax.rem(r, owned) * each + lax.div(r, per_k),
    )
    wide_f32[...] = jnp.zeros_like(wide_f32)
    each_of(w_count, lambda d: first_copy(d).wait_recv())
    picked = dot(pick, first_buf[...].reshape(w_count * SLOT, orbitals))
    for i in range(each):
        wide_f32[:, i * orbitals : (i + 1) * orbitals] = picked[i * per_k : (i + 1) * per_k, :]
    entries[k] = wide_f32[...].astype(BF16)
    gather = Gather(entries, entry_sems, per_k)
    gather.begin()
    hr_copy.wait_recv()
    gather.middle(second_window)
    for src, slots in gather.late():
        gather.wait_late(src, slots)
    sums = dot(entries[...].reshape(rows, entries.shape[-1]), hr_buf[...].reshape(2 * gp, entries.shape[-1]), ((1,), (1,)))
    partial[...] = packed(sums, per_w)

    def partial_copy(d):
        dst = to_w(d)
        return remote(partial.at[block(dst, side)], partial_in.at[w], partial_sems, d, at_w(dst))

    start_each(w_count, partial_copy)
    third_window()
    partial_in[w] = partial[block(w, side)]
    finish_first_window()
    aux_copy.wait_recv()
    aux = jnp.concatenate([aux_buf[0], aux_buf[1]], axis=1)
    each_of(w_count, lambda d: partial_copy(d).wait_recv())
    bias = jnp.sum(partial_in[...], axis=0)
    piece_b[...] = bias
    piece_f[...] = (aux - unpacked(bias[None])).astype(BF16)

    def field_copy(d):
        dst = to_w(d)
        return remote(piece_f, chip_fields.at[span(block(w, lax.div(dst, ring)), per_w)], field_w_sems, d, at_w(dst))

    start_each(w_count, field_copy)
    chip_fields[span(block(w, side), per_w), :] = piece_f[...]

    def bias_copy(d):
        return remote(piece_b, bias_in.at[w], bias_sems, d, at_w(to_w(d)))

    each_of(w_count, lambda d: field_copy(d).wait_recv())
    fields[k] = packed(chip_fields[...], rows)[0]
    gather = Gather(fields, field_c_sems, fields.shape[1])
    gather.begin()
    bias_in[w] = piece_b[...]
    gather.middle(lambda: start_each(w_count, bias_copy))
    finish_others()

    def term(kk, columns):
        return dot(whole_fields[kk], vecs_buf[kk, :, :, columns].reshape(2 * gp, part_width))

    def hop1(d, n):
        dst = to_k(d)
        return remote(out.at[n, span(dst, per_k)], one_in.at[n, k], hop1_sems, n * k_count + d, at_k(dst))

    def hop2(d, n):
        dst = to_w(d)
        return remote(two_out.at[n, span(dst, per_w)], result_ref.at[n, w], hop2_sems, n * w_count + d, at_near(dst))

    regroup = permutation(rows, rows, lambda r: lax.rem(lax.div(r, owned), k_count) * per_k + lax.div(r, per_w) * owned + lax.rem(r, owned))

    def own_result(n):
        return pltpu.make_async_copy(two_out.at[n, span(w, per_w)], result_ref.at[n, w], load_sems.at[5 + n])

    for step in range(CHUNKS + LAG):
        n = step
        if n < CHUNKS:
            columns = slice(n * part_width, (n + 1) * part_width)
            total = None
            for kk in (k, back, fore, back_x, fore_x, across, half, half_x):
                if n == 0:
                    vec_from_sibling(kk).wait_recv()
                    for src, slots in gather.late():
                        if kk is src:
                            gather.wait_late(src, slots)
                    whole_fields[kk] = unpacked(fields[kk][None])
                total = term(kk, columns) if total is None else total + term(kk, columns)
            out[n] = total.astype(BF16)
            start_each(k_count, functools.partial(hop1, n=n))
            one_in[n, k] = out[n, span(k, per_k), :]
        n = step - LAG
        if n >= 0:
            each_of(k_count, lambda d: hop1(d, n).wait_recv())
            two_out[n] = dot(regroup, one_in[n].reshape(rows, part_width)).astype(BF16)
            start_each(w_count, functools.partial(hop2, n=n))
            own_result(n).start()

    each_of(w_count, lambda d: bias_copy(d).wait_recv())
    sums = unpacked(bias_in[...])
    low, high = sums[:, :gp], sums[:, gp:]
    bias_out[...] = jnp.where(core == 0, high, low)
    sib_copy = start(remote(bias_out, bias_sib, one_sems, 2, sibling))

    def spread(which):
        shape = (rows, bias_ref.shape[1])
        return jnp.where(iota(shape, 1) == walker_of(iota(shape, 0), which), 1.0, 0.0)

    mine = dot(jnp.where(core == 0, low, high), spread(core), ((0,), (0,)), HIGH)
    sib_copy.wait_recv()
    theirs = dot(bias_sib[...], spread(other), ((0,), (0,)), HIGH)
    bias_ref[...] = (mine + theirs)[:vec_count]
    bias_write = pltpu.make_async_copy(bias_ref, bias_hbm, load_sems.at[5 + CHUNKS])
    bias_write.start()

    for n in range(CHUNKS):
        each_of(w_count, lambda d: hop2(d, n).wait_recv())
        own_result(n).wait()
    bias_write.wait()
    for drain in drains:
        drain()


def taylor_kernel(k_count, walkers_hbm, pieces_hbm, bias_hbm, out_ref, bias_out, walkers_ref, pieces_ref, flat, stacked, sems):
    pairs = ((pieces_hbm, pieces_ref), (walkers_hbm, walkers_ref), (bias_hbm, bias_out))
    copies = [pltpu.make_async_copy(src, dst, sems.at[n]) for n, (src, dst) in enumerate(pairs)]
    for copy in copies:
        copy.start()
    owned, _, orbitals = walkers_ref.shape
    chunks, w_count, per_w, part_width = pieces_ref.shape
    width = chunks * part_width
    each = orbitals // w_count
    rows = w_count * per_w
    order = permutation(
        rows, rows, lambda r: lax.rem(r, w_count) * per_w + lax.rem(lax.div(r, w_count), k_count) * owned + lax.div(r, w_count * k_count)
    )
    for copy in copies[:2]:
        copy.wait()
    sorted_ = [dot(order, pieces_ref[n].reshape(rows, part_width)) for n in range(chunks)]
    place = permutation(orbitals, orbitals, lambda r: lax.rem(r, each) * w_count + lax.div(r, each))
    terms, totals, onebody = [], [], []
    for j in range(owned):
        for kk in range(k_count):
            at = (j * k_count + kk) * w_count
            for n in range(chunks):
                lane = kk * width + n * part_width
                flat[j, :, lane : lane + part_width] = sorted_[n][at : at + w_count, :]
        for q in range(each):
            stacked[j, q * w_count : (q + 1) * w_count, :] = flat[j, :, q * orbitals : (q + 1) * orbitals].astype(BF16)
        onebody.append(dot(stacked[j], place, ((0,), (1,))).astype(BF16))
        terms.append(walkers_ref[j])
        totals.append(walkers_ref[j])
    for step in range(1, TAYLOR + 1):
        for j in range(owned):
            head = terms[j].astype(BF16)
            rest = (terms[j] - head.astype(F32)).astype(BF16)
            both = dot(jnp.concatenate([head, rest], axis=0), onebody[j])
            terms[j] = (both[: head.shape[0]] + both[head.shape[0] :]) * (-1.0 / step)
            totals[j] = totals[j] + terms[j]
    for j in range(owned):
        out_ref[j] = totals[j]
    copies[2].wait()


def body(trial, walkers, aux_field, half_rotated, cholesky_vecs):
    k_count = lax.axis_size("chol") // 2
    w_count = lax.axis_size("walk")
    assert k_count == SIDE * LINE and w_count == SIDE * k_count and 256 < 2 * up(half_rotated.shape[0], 32) == 320
    owned, electrons, orbitals = walkers.shape
    vec_count, local_entries = half_rotated.shape
    walker_count = aux_field.shape[0]
    local_pairs = cholesky_vecs.shape[1]
    each = electrons // w_count
    gp = up(vec_count, 32)
    lanes = up(local_entries, 128)
    width = up(-(-local_pairs // k_count), 128 * CHUNKS)
    part_width = width // CHUNKS
    rows = k_count * w_count * owned
    per_k, per_w = w_count * owned, k_count * owned
    vmem = pl.BlockSpec(memory_space=pltpu.VMEM)
    hbm = pl.BlockSpec(memory_space=pltpu.HBM)
    dma = pltpu.SemaphoreType.DMA
    pieces, force_bias = pl.pallas_call(
        functools.partial(exchange_kernel, (k_count, w_count, owned, each, orbitals, vec_count)),
        out_shape=(
            jax.ShapeDtypeStruct((CHUNKS, w_count, per_w, part_width), BF16),
            jax.ShapeDtypeStruct((vec_count, walker_count), F32),
        ),
        in_specs=[hbm] * 5,
        out_specs=(hbm, hbm),
        scratch_shapes=[
            pltpu.VMEM(trial.shape, F32),
            pltpu.VMEM(walkers.shape, F32),
            pltpu.VMEM((vec_count, walker_count), F32),
            pltpu.VMEM(cholesky_vecs.shape, BF16),
            pltpu.VMEM(half_rotated.shape, BF16),
            pltpu.VMEM((vec_count, walker_count), F32),
            pltpu.VMEM((w_count * SLOT, orbitals), BF16),
            pltpu.VMEM((2, gp, lanes), BF16),
            pltpu.VMEM((per_w, gp), F32),
            pltpu.VMEM((2, per_w, gp), F32),
            pltpu.VMEM((gp, k_count * width), BF16),
            pltpu.VMEM((k_count, 2, gp, width), BF16),
            pltpu.VMEM((2, gp // 2, width), BF16),
            pltpu.VMEM((w_count, SLOT, orbitals), BF16),
            pltpu.VMEM((per_k, lanes), F32),
            pltpu.VMEM((k_count, per_k, lanes), BF16),
            pltpu.VMEM((w_count, per_w * 5 // 2, 128), F32),
            pltpu.VMEM((w_count, per_w * 5 // 2, 128), F32),
            pltpu.VMEM((per_w, 2 * gp), BF16),
            pltpu.VMEM((per_w * 5 // 2, 128), F32),
            pltpu.VMEM((rows, 2 * gp), BF16),
            pltpu.VMEM((k_count, rows * 5 // 2, 128), BF16),
            pltpu.VMEM((k_count, rows, 2 * gp), BF16),
            pltpu.VMEM((w_count, per_w * 5 // 2, 128), F32),
            pltpu.VMEM((rows, gp), F32),
            pltpu.VMEM((rows, gp), F32),
            pltpu.VMEM((CHUNKS, rows, part_width), BF16),
            pltpu.VMEM((CHUNKS, k_count, per_k, part_width), BF16),
            pltpu.VMEM((CHUNKS, rows, part_width), BF16),
            dma((6 + CHUNKS,)),
            dma((3, 3)),
            dma((2, 11)),
            dma((2, k_count)),
            dma((2, w_count)),
            dma((2, 9)),
            dma((2, w_count)),
            dma((2, w_count)),
            dma((2, 9)),
            dma((2, w_count)),
            dma((2, CHUNKS * k_count)),
            dma((2, CHUNKS * w_count)),
        ],
        compiler_params=pltpu.CompilerParams(collective_id=0, has_side_effects=True, vmem_limit_bytes=VMEM_BYTES),
    )(trial, walkers, half_rotated, aux_field.T, cholesky_vecs)

    next_walkers, force_bias = pl.pallas_call(
        functools.partial(taylor_kernel, k_count),
        out_shape=(jax.ShapeDtypeStruct(walkers.shape, F32), jax.ShapeDtypeStruct(force_bias.shape, F32)),
        in_specs=[hbm, hbm, hbm],
        out_specs=(vmem, vmem),
        scratch_shapes=[
            pltpu.VMEM(walkers.shape, F32),
            pltpu.VMEM(pieces.shape, BF16),
            pltpu.VMEM((owned, w_count, k_count * width), F32),
            pltpu.VMEM((owned, orbitals, orbitals), BF16),
            dma((3,)),
        ],
        compiler_params=pltpu.CompilerParams(vmem_limit_bytes=VMEM_BYTES),
    )(walkers, pieces, force_bias)
    return (next_walkers, force_bias.T)


def solution(mesh):
    in_specs = (
        P(),
        P(("chol", "walk"), None, None),
        P(None, "chol"),
        P("chol", "walk"),
        P("chol", "walk"),
    )
    out_specs = (P(("chol", "walk"), None, None), P(None, "chol"))
    return jax.shard_map(body, mesh=mesh, in_specs=in_specs, out_specs=out_specs, check_vma=False)
```

```python
import functools

import jax
import jax.numpy as jnp
from jax import lax
from jax.experimental import pallas as pl
from jax.experimental.pallas import tpu as pltpu
from jax.sharding import PartitionSpec as P

TAYLOR = 6
SIDE, LINE = 2, 4
CHUNKS = 5
LAG = 3
HIGH = lax.Precision.HIGHEST
MESH = pl.DeviceIdType.MESH
F32 = jnp.float32
BF16 = jnp.bfloat16
VMEM_BYTES = 62 * 1024 * 1024
SLOT = 16


def up(value, multiple):
    return -(-value // multiple) * multiple


def iota(shape, dim):
    return lax.broadcasted_iota(jnp.int32, shape, dim)


def permutation(rows, cols, source):
    return jnp.where(iota((rows, cols), 1) == source(iota((rows, cols), 0)), 1.0, 0.0).astype(BF16)


def dot(a, b, contract=((1,), (0,)), precision=None):
    return lax.dot_general(a, b, (contract, ((), ())), preferred_element_type=F32, precision=precision)


def packed(value, block):
    rows = value.shape[0]
    tail = value[:, 256:].reshape(rows // block, 2, block // 2, 64)
    tail = jnp.concatenate([tail[:, 0], tail[:, 1]], axis=-1)
    parts = [value[:, :128].reshape(-1, block, 128), value[:, 128:256].reshape(-1, block, 128), tail]
    return jnp.concatenate(parts, axis=1)


def unpacked(value):
    block = value.shape[1] * 2 // 5
    tail = value[:, 2 * block :]
    tail = jnp.concatenate([tail[..., :64], tail[..., 64:]], axis=1)
    parts = [value[:, :block], value[:, block : 2 * block], tail]
    return jnp.concatenate(parts, axis=-1).reshape(-1, 320)


def invert(grams):
    size = grams[0].shape[0]
    rows = iota((size, size), 0)
    lanes = iota((1, size), 1)

    def pair(a, k):
        one = jnp.broadcast_to(a[:, k : k + 1], (size, size))
        two = jnp.broadcast_to(a[:, k + 1 : k + 2], (size, size))
        e11, e21, e12, e22 = one[k : k + 1], one[k + 1 : k + 2], two[k : k + 1], two[k + 1 : k + 2]
        first = 1.0 / e11
        right, below = first * e12, e21 * first
        p22 = 1.0 / (e22 - below * e12)
        p12, p21 = -right * p22, -p22 * below
        p11 = first + right * p22 * below
        upper = jnp.where(lanes == k, 1.0, jnp.where(lanes == k + 1, 0.0, a[k : k + 1]))
        lower = jnp.where(lanes == k, 0.0, jnp.where(lanes == k + 1, 1.0, a[k + 1 : k + 2]))
        upper, lower = p11 * upper + p12 * lower, p21 * upper + p22 * lower
        kept = jnp.where((lanes == k) | (lanes == k + 1), 0.0, a)
        return jnp.where(rows == k, upper, jnp.where(rows == k + 1, lower, kept - one * upper - two * lower))

    for k in range(0, size, 2):
        grams = [pair(a, k) for a in grams]
    return grams


def blocks_of_green(parts, trial_ref, walkers_ref, before_inverse):
    count, electrons, _ = walkers_ref.shape
    each = electrons // parts
    trial = trial_ref[...]
    walkers = [walkers_ref[j] for j in range(count)]
    corr = [dot(trial, w, ((1,), (1,)), HIGH) for w in walkers]
    grams = [dot(c, c, ((1,), (1,)), HIGH) for c in corr]
    rhs = [dot(c, w, precision=HIGH) for c, w in zip(corr, walkers)]
    before_inverse()
    inverse = invert(grams)
    green = [dot(g, r, precision=HIGH).astype(BF16) for g, r in zip(inverse, rhs)]
    total = None
    for j in range(count):

        def source(r):
            inside = r % SLOT - each * j
            return jnp.where((inside >= 0) & (inside < each), (r // SLOT) * each + inside, -1)

        part = dot(permutation(parts * SLOT, electrons, source), green[j])
        total = part if total is None else total + part
    return total.astype(BF16)


def exchange_kernel(
    dims,
    trial_hbm,
    walkers_hbm,
    hr_hbm,
    aux_hbm,
    vecs_hbm,
    result_ref,
    bias_hbm,
    trial_ref,
    walkers_ref,
    aux_ref,
    vecs_ref,
    hr_ref,
    bias_ref,
    green,
    hr_buf,
    aux_out,
    aux_buf,
    vecs_out,
    vecs_buf,
    relay,
    first_buf,
    wide_f32,
    entries,
    partial,
    partial_in,
    piece_f,
    piece_b,
    chip_fields,
    fields,
    whole_fields,
    bias_in,
    bias_out,
    bias_sib,
    out,
    one_in,
    two_out,
    load_sems,
    one_sems,
    vec_sems,
    fwd_sems,
    first_sems,
    entry_sems,
    partial_sems,
    field_w_sems,
    field_c_sems,
    bias_sems,
    hop1_sems,
    hop2_sems,
):
    k_count, w_count, owned, each, orbitals, vec_count = dims
    c = lax.axis_index("chol")
    w = lax.axis_index("walk")
    core = lax.rem(c, 2)
    k = lax.div(c, 2)
    other = 1 - core
    sibling = (2 * k + other, w)
    gp = hr_buf.shape[1]
    width = vecs_buf.shape[-1]
    part_width = width // CHUNKS
    rows = k_count * w_count * owned
    per_k = w_count * owned
    per_w = k_count * owned
    local_pairs = vecs_ref.shape[1]
    local_entries = hr_ref.shape[1]

    line = LINE * lax.div(k, LINE)
    across = lax.rem(k + LINE, k_count)
    line_across = lax.rem(line + LINE, k_count)

    def along(start, step):
        return start + lax.rem(k - line + step, LINE)

    fore, back, half = along(line, 1), along(line, LINE - 1), along(line, 2)
    fore_x, back_x, half_x = along(line_across, 1), along(line_across, LINE - 1), along(line_across, 2)

    def at_k(kk):
        return (2 * kk + core, w)

    def at_w(ww):
        return (c, ww)

    ring = w_count // SIDE
    side = lax.div(w, ring)

    def at_near(ww):
        return (2 * jnp.where(lax.div(ww, ring) == side, k, across) + core, ww)

    def block(piece, on_side):
        kk = lax.div(piece, SIDE)
        return SIDE * jnp.where(lax.rem(piece, SIDE) == on_side, kk, lax.rem(kk + LINE, k_count)) + lax.rem(piece, SIDE)

    def remote(src, dst, sems, slot, device):
        return pltpu.make_async_remote_copy(
            src_ref=src, dst_ref=dst, send_sem=sems.at[0, slot], recv_sem=sems.at[1, slot], device_id=device, device_id_type=MESH
        )

    drains = []

    def start(copy):
        copy.start()
        drains.append(copy.wait_send)
        return copy

    def each_of(count, body, first=1):
        def step(d, carry):
            body(d)
            return carry

        lax.fori_loop(first, count, step, 0)

    def start_each(count, make):
        each_of(count, lambda d: make(d).start())
        drains.append(lambda: each_of(count, lambda d: make(d).wait_send()))

    def to_k(d):
        return lax.rem(k + d, k_count)

    def to_w(d):
        return lax.rem(w + d, w_count)

    def walker_of(row, which):
        return per_k * (2 * lax.div(row, per_k) + which) + lax.rem(row, per_k)

    def span(index, size):
        return pl.ds(pl.multiple_of(index * size, size), size)

    pairs = ((trial_hbm, trial_ref), (walkers_hbm, walkers_ref), (aux_hbm, aux_ref), (vecs_hbm, vecs_ref), (hr_hbm, hr_ref))
    load_trial, load_walkers, load_aux, load_vecs, load_hr = loads = [
        pltpu.make_async_copy(src, dst, load_sems.at[n]) for n, (src, dst) in enumerate(pairs)
    ]
    for load in loads:
        load.start()

    barrier = pltpu.get_barrier_semaphore()
    each_of(k_count, lambda d: pl.semaphore_signal(barrier, inc=1, device_id=at_k(to_k(d)), device_id_type=MESH))
    each_of(w_count, lambda d: pl.semaphore_signal(barrier, inc=1, device_id=at_w(to_w(d)), device_id_type=MESH))
    opposite = ring * (SIDE - 1 - side)
    each_of(ring, lambda d: pl.semaphore_signal(barrier, inc=1, device_id=at_near(opposite + d), device_id_type=MESH), 0)
    pl.semaphore_signal(barrier, inc=1, device_id=sibling, device_id_type=MESH)

    def pad_vectors():
        edge = local_pairs // 128 * 128
        vecs_out[gp - 16 :, :] = jnp.zeros((16, vecs_out.shape[1]), BF16)
        if edge < vecs_out.shape[1]:
            vecs_out[:, edge:] = jnp.zeros((gp, vecs_out.shape[1] - edge), BF16)
        load_vecs.wait()
        vecs_out[:vec_count, :local_pairs] = vecs_ref[...]
        hr_buf[core] = jnp.zeros(hr_buf.shape[1:], BF16)
        load_hr.wait()
        hr_buf[core, :vec_count, :local_entries] = hr_ref[...]

    cut = gp // 2
    lower, upper = pl.ds(0, cut), pl.ds(cut, gp - cut)

    def vec_full(slot, dst, src):
        return remote(vecs_out.at[:, span(dst, width)], vecs_buf.at[src, core], vec_sems, slot, at_k(dst))

    def vec_lower(slot, dst, src):
        return remote(vecs_out.at[lower, span(dst, width)], vecs_buf.at[src, core, lower], vec_sems, slot, at_k(dst))

    def vec_relay(slot, dst, by):
        return remote(vecs_out.at[upper, span(dst, width)], relay.at[slot - 7], vec_sems, slot, at_k(by))

    def vec_upper(slot, dst, src):
        return remote(relay.at[slot - 9], vecs_buf.at[src, core, upper], vec_sems, slot, at_k(dst))

    def vec_forward(kk):
        return remote(vecs_buf.at[kk, core], vecs_buf.at[kk, core], fwd_sems, kk, sibling)

    def vec_from_sibling(kk):
        return remote(vecs_buf.at[kk, other], vecs_buf.at[kk, other], fwd_sems, kk, sibling)

    own_vecs = pltpu.make_async_copy(vecs_out.at[:, span(k, width)], vecs_buf.at[k, core], one_sems.at[2, 0])
    hr_copy = remote(hr_buf.at[core], hr_buf.at[core], one_sems, 0, sibling)
    aux_copy = remote(aux_out, aux_buf.at[core], one_sems, 1, sibling)

    def first_window():
        pad_vectors()
        pl.semaphore_wait(barrier, k_count + w_count - 1 + ring)
        start(vec_relay(7, half, back))
        start(vec_relay(8, half_x, back))
        start(vec_full(0, fore, k))
        start(vec_full(1, back, k))
        start(vec_full(3, fore_x, k))
        start(vec_full(4, back_x, k))
        own_vecs.start()
        start(hr_copy)

    def second_window():
        start(vec_full(2, across, k))

    def third_window():
        start(vec_lower(5, half, k))
        start(vec_lower(6, half_x, k))
        vec_relay(7, half, back).wait_recv()
        start(vec_upper(9, back, fore))
        vec_relay(8, half_x, back).wait_recv()
        start(vec_upper(10, back_x, fore))

    def finish_first_window():
        own_vecs.wait()
        start(vec_forward(k))
        for slot, src in ((0, back), (1, fore), (3, back_x), (4, fore_x), (2, across)):
            vec_full(slot, k, src).wait_recv()
            start(vec_forward(src))

    def finish_others():
        for slots, src in (((5, 9), half), ((6, 10), half_x)):
            vec_lower(slots[0], k, src).wait_recv()
            vec_upper(slots[1], k, src).wait_recv()
            start(vec_forward(src))

    class Gather:
        def __init__(self, buf, sems, size):
            self.buf, self.sems = buf, sems
            self.halves = pl.ds(0, size // 2), pl.ds(size // 2, size - size // 2)

        def full(self, slot, src, dst):
            return remote(self.buf.at[src], self.buf.at[src], self.sems, slot, at_k(dst))

        def part(self, slot, src, dst):
            ref = self.buf.at[src, self.halves[slot % 2]]
            return remote(ref, ref, self.sems, slot, at_k(dst))

        def begin(self):
            start(self.full(8, k, across))
            start(self.full(0, k, fore))
            start(self.full(1, k, back))

        def middle(self, then=lambda: None):
            self.full(8, across, across).wait_recv()
            start(self.full(2, across, fore))
            start(self.full(3, across, back))
            then()
            self.full(0, back, fore).wait_recv()
            start(self.part(4, back, fore))
            self.full(1, fore, back).wait_recv()
            start(self.part(5, fore, back))
            self.full(2, back_x, fore).wait_recv()
            start(self.part(6, back_x, fore))
            self.full(3, fore_x, back).wait_recv()
            start(self.part(7, fore_x, back))

        def late(self):
            return ((half, (4, 5)), (half_x, (6, 7)))

        def wait_late(self, src, slots):
            for slot in slots:
                self.part(slot, src, fore).wait_recv()

    load_trial.wait()
    load_walkers.wait()
    green[...] = blocks_of_green(w_count, trial_ref, walkers_ref, first_window)

    def first_copy(d):
        dst = to_w(d)
        return remote(green.at[span(dst, SLOT)], first_buf.at[w], first_sems, d, at_near(dst))

    start_each(w_count, first_copy)
    first_buf[w] = green[span(w, SLOT), :]

    def aux_piece(which):
        shape = (per_w, aux_ref.shape[1])
        pick = jnp.where(iota(shape, 1) == walker_of(iota(shape, 0) + per_w * w, which), 1.0, 0.0)
        return dot(pick, aux_ref[...], ((1,), (1,)), HIGH)

    load_aux.wait()
    aux_out[...] = jnp.zeros_like(aux_out)
    aux_out[:, :vec_count] = aux_piece(other)
    start(aux_copy)
    aux_buf[core] = jnp.zeros(aux_buf.shape[1:], F32)
    aux_buf[core, :, :vec_count] = aux_piece(core)

    pick = permutation(
        each * per_k,
        w_count * SLOT,
        lambda r: lax.rem(r, per_k) // owned * SLOT + lax.rem(r, owned) * each + lax.div(r, per_k),
    )
    wide_f32[...] = jnp.zeros_like(wide_f32)
    each_of(w_count, lambda d: first_copy(d).wait_recv())
    picked = dot(pick, first_buf[...].reshape(w_count * SLOT, orbitals))
    for i in range(each):
        wide_f32[:, i * orbitals : (i + 1) * orbitals] = picked[i * per_k : (i + 1) * per_k, :]
    entries[k] = wide_f32[...].astype(BF16)
    gather = Gather(entries, entry_sems, per_k)
    gather.begin()
    hr_copy.wait_recv()
    gather.middle(second_window)
    for src, slots in gather.late():
        gather.wait_late(src, slots)
    sums = dot(entries[...].reshape(rows, entries.shape[-1]), hr_buf[...].reshape(2 * gp, entries.shape[-1]), ((1,), (1,)))
    partial[...] = packed(sums, per_w)

    def partial_copy(d):
        dst = to_w(d)
        return remote(partial.at[block(dst, side)], partial_in.at[w], partial_sems, d, at_w(dst))

    start_each(w_count, partial_copy)
    third_window()
    partial_in[w] = partial[block(w, side)]
    aux_copy.wait_recv()
    aux = jnp.concatenate([aux_buf[0], aux_buf[1]], axis=1)
    each_of(w_count, lambda d: partial_copy(d).wait_recv())
    bias = jnp.sum(partial_in[...], axis=0)
    piece_b[...] = bias
    piece_f[...] = (aux - unpacked(bias[None])).astype(BF16)

    def field_copy(d):
        dst = to_w(d)
        return remote(piece_f, chip_fields.at[span(block(w, lax.div(dst, ring)), per_w)], field_w_sems, d, at_w(dst))

    start_each(w_count, field_copy)
    finish_first_window()
    chip_fields[span(block(w, side), per_w), :] = piece_f[...]

    def bias_copy(d):
        return remote(piece_b, bias_in.at[w], bias_sems, d, at_w(to_w(d)))

    each_of(w_count, lambda d: field_copy(d).wait_recv())
    fields[k] = packed(chip_fields[...], rows)[0]
    gather = Gather(fields, field_c_sems, fields.shape[1])
    gather.begin()
    bias_in[w] = piece_b[...]
    gather.middle(lambda: start_each(w_count, bias_copy))
    finish_others()

    def term(kk, columns):
        return dot(whole_fields[kk], vecs_buf[kk, :, :, columns].reshape(2 * gp, part_width))

    def hop1(d, n):
        dst = to_k(d)
        return remote(out.at[n, span(dst, per_k)], one_in.at[n, k], hop1_sems, n * k_count + d, at_k(dst))

    def hop2(d, n):
        dst = to_w(d)
        return remote(two_out.at[n, span(dst, per_w)], result_ref.at[n, w], hop2_sems, n * w_count + d, at_near(dst))

    regroup = permutation(rows, rows, lambda r: lax.rem(lax.div(r, owned), k_count) * per_k + lax.div(r, per_w) * owned + lax.rem(r, owned))

    def own_result(n):
        return pltpu.make_async_copy(two_out.at[n, span(w, per_w)], result_ref.at[n, w], load_sems.at[5 + n])

    for step in range(CHUNKS + LAG):
        n = step
        if n < CHUNKS:
            columns = slice(n * part_width, (n + 1) * part_width)
            total = None
            for kk in (k, back, fore, back_x, fore_x, across, half, half_x):
                if n == 0:
                    vec_from_sibling(kk).wait_recv()
                    for src, slots in gather.late():
                        if kk is src:
                            gather.wait_late(src, slots)
                    whole_fields[kk] = unpacked(fields[kk][None])
                total = term(kk, columns) if total is None else total + term(kk, columns)
            out[n] = total.astype(BF16)
            start_each(k_count, functools.partial(hop1, n=n))
            one_in[n, k] = out[n, span(k, per_k), :]
        n = step - LAG
        if n >= 0:
            each_of(k_count, lambda d: hop1(d, n).wait_recv())
            two_out[n] = dot(regroup, one_in[n].reshape(rows, part_width)).astype(BF16)
            start_each(w_count, functools.partial(hop2, n=n))
            own_result(n).start()

    each_of(w_count, lambda d: bias_copy(d).wait_recv())
    sums = unpacked(bias_in[...])
    low, high = sums[:, :gp], sums[:, gp:]
    bias_out[...] = jnp.where(core == 0, high, low)
    sib_copy = start(remote(bias_out, bias_sib, one_sems, 2, sibling))

    def spread(which):
        shape = (rows, bias_ref.shape[1])
        return jnp.where(iota(shape, 1) == walker_of(iota(shape, 0), which), 1.0, 0.0)

    mine = dot(jnp.where(core == 0, low, high), spread(core), ((0,), (0,)), HIGH)
    sib_copy.wait_recv()
    theirs = dot(bias_sib[...], spread(other), ((0,), (0,)), HIGH)
    bias_ref[...] = (mine + theirs)[:vec_count]
    bias_write = pltpu.make_async_copy(bias_ref, bias_hbm, load_sems.at[5 + CHUNKS])
    bias_write.start()

    for n in range(CHUNKS):
        each_of(w_count, lambda d: hop2(d, n).wait_recv())
        own_result(n).wait()
    bias_write.wait()
    for drain in drains:
        drain()


def taylor_kernel(k_count, walkers_hbm, pieces_hbm, bias_hbm, out_ref, bias_out, walkers_ref, pieces_ref, flat, stacked, sems):
    pairs = ((pieces_hbm, pieces_ref), (walkers_hbm, walkers_ref), (bias_hbm, bias_out))
    copies = [pltpu.make_async_copy(src, dst, sems.at[n]) for n, (src, dst) in enumerate(pairs)]
    for copy in copies:
        copy.start()
    owned, _, orbitals = walkers_ref.shape
    chunks, w_count, per_w, part_width = pieces_ref.shape
    width = chunks * part_width
    each = orbitals // w_count
    rows = w_count * per_w
    order = permutation(
        rows, rows, lambda r: lax.rem(r, w_count) * per_w + lax.rem(lax.div(r, w_count), k_count) * owned + lax.div(r, w_count * k_count)
    )
    for copy in copies[:2]:
        copy.wait()
    sorted_ = [dot(order, pieces_ref[n].reshape(rows, part_width)) for n in range(chunks)]
    place = permutation(orbitals, orbitals, lambda r: lax.rem(r, each) * w_count + lax.div(r, each))
    terms, totals, onebody = [], [], []
    for j in range(owned):
        for kk in range(k_count):
            at = (j * k_count + kk) * w_count
            for n in range(chunks):
                lane = kk * width + n * part_width
                flat[j, :, lane : lane + part_width] = sorted_[n][at : at + w_count, :]
        for q in range(each):
            stacked[j, q * w_count : (q + 1) * w_count, :] = flat[j, :, q * orbitals : (q + 1) * orbitals].astype(BF16)
        onebody.append(dot(stacked[j], place, ((0,), (1,))).astype(BF16))
        terms.append(walkers_ref[j])
        totals.append(walkers_ref[j])
    for step in range(1, TAYLOR + 1):
        for j in range(owned):
            head = terms[j].astype(BF16)
            rest = (terms[j] - head.astype(F32)).astype(BF16)
            both = dot(jnp.concatenate([head, rest], axis=0), onebody[j])
            terms[j] = (both[: head.shape[0]] + both[head.shape[0] :]) * (-1.0 / step)
            totals[j] = totals[j] + terms[j]
    for j in range(owned):
        out_ref[j] = totals[j]
    copies[2].wait()


def body(trial, walkers, aux_field, half_rotated, cholesky_vecs):
    k_count = lax.axis_size("chol") // 2
    w_count = lax.axis_size("walk")
    assert k_count == SIDE * LINE and w_count == SIDE * k_count and 256 < 2 * up(half_rotated.shape[0], 32) == 320
    owned, electrons, orbitals = walkers.shape
    vec_count, local_entries = half_rotated.shape
    walker_count = aux_field.shape[0]
    local_pairs = cholesky_vecs.shape[1]
    each = electrons // w_count
    gp = up(vec_count, 32)
    lanes = up(local_entries, 128)
    width = up(-(-local_pairs // k_count), 128 * CHUNKS)
    part_width = width // CHUNKS
    rows = k_count * w_count * owned
    per_k, per_w = w_count * owned, k_count * owned
    vmem = pl.BlockSpec(memory_space=pltpu.VMEM)
    hbm = pl.BlockSpec(memory_space=pltpu.HBM)
    dma = pltpu.SemaphoreType.DMA
    pieces, force_bias = pl.pallas_call(
        functools.partial(exchange_kernel, (k_count, w_count, owned, each, orbitals, vec_count)),
        out_shape=(
            jax.ShapeDtypeStruct((CHUNKS, w_count, per_w, part_width), BF16),
            jax.ShapeDtypeStruct((vec_count, walker_count), F32),
        ),
        in_specs=[hbm] * 5,
        out_specs=(hbm, hbm),
        scratch_shapes=[
            pltpu.VMEM(trial.shape, F32),
            pltpu.VMEM(walkers.shape, F32),
            pltpu.VMEM((vec_count, walker_count), F32),
            pltpu.VMEM(cholesky_vecs.shape, BF16),
            pltpu.VMEM(half_rotated.shape, BF16),
            pltpu.VMEM((vec_count, walker_count), F32),
            pltpu.VMEM((w_count * SLOT, orbitals), BF16),
            pltpu.VMEM((2, gp, lanes), BF16),
            pltpu.VMEM((per_w, gp), F32),
            pltpu.VMEM((2, per_w, gp), F32),
            pltpu.VMEM((gp, k_count * width), BF16),
            pltpu.VMEM((k_count, 2, gp, width), BF16),
            pltpu.VMEM((2, gp // 2, width), BF16),
            pltpu.VMEM((w_count, SLOT, orbitals), BF16),
            pltpu.VMEM((per_k, lanes), F32),
            pltpu.VMEM((k_count, per_k, lanes), BF16),
            pltpu.VMEM((w_count, per_w * 5 // 2, 128), F32),
            pltpu.VMEM((w_count, per_w * 5 // 2, 128), F32),
            pltpu.VMEM((per_w, 2 * gp), BF16),
            pltpu.VMEM((per_w * 5 // 2, 128), F32),
            pltpu.VMEM((rows, 2 * gp), BF16),
            pltpu.VMEM((k_count, rows * 5 // 2, 128), BF16),
            pltpu.VMEM((k_count, rows, 2 * gp), BF16),
            pltpu.VMEM((w_count, per_w * 5 // 2, 128), F32),
            pltpu.VMEM((rows, gp), F32),
            pltpu.VMEM((rows, gp), F32),
            pltpu.VMEM((CHUNKS, rows, part_width), BF16),
            pltpu.VMEM((CHUNKS, k_count, per_k, part_width), BF16),
            pltpu.VMEM((CHUNKS, rows, part_width), BF16),
            dma((6 + CHUNKS,)),
            dma((3, 3)),
            dma((2, 11)),
            dma((2, k_count)),
            dma((2, w_count)),
            dma((2, 9)),
            dma((2, w_count)),
            dma((2, w_count)),
            dma((2, 9)),
            dma((2, w_count)),
            dma((2, CHUNKS * k_count)),
            dma((2, CHUNKS * w_count)),
        ],
        compiler_params=pltpu.CompilerParams(collective_id=0, has_side_effects=True, vmem_limit_bytes=VMEM_BYTES),
    )(trial, walkers, half_rotated, aux_field.T, cholesky_vecs)

    next_walkers, force_bias = pl.pallas_call(
        functools.partial(taylor_kernel, k_count),
        out_shape=(jax.ShapeDtypeStruct(walkers.shape, F32), jax.ShapeDtypeStruct(force_bias.shape, F32)),
        in_specs=[hbm, hbm, hbm],
        out_specs=(vmem, vmem),
        scratch_shapes=[
            pltpu.VMEM(walkers.shape, F32),
            pltpu.VMEM(pieces.shape, BF16),
            pltpu.VMEM((owned, w_count, k_count * width), F32),
            pltpu.VMEM((owned, orbitals, orbitals), BF16),
            dma((3,)),
        ],
        compiler_params=pltpu.CompilerParams(vmem_limit_bytes=VMEM_BYTES),
    )(walkers, pieces, force_bias)
    return (next_walkers, force_bias.T)


def solution(mesh):
    in_specs = (
        P(),
        P(("chol", "walk"), None, None),
        P(None, "chol"),
        P("chol", "walk"),
        P("chol", "walk"),
    )
    out_specs = (P(("chol", "walk"), None, None), P(None, "chol"))
    return jax.shard_map(body, mesh=mesh, in_specs=in_specs, out_specs=out_specs, check_vma=False)
```
